256 devices in a mesh: rows: 8 (over x, core), wide: 32 (over z, y).
Axes of the slice: x: 4, y: 4, z: 8, core: 2. Of those that a mesh axis runs over, the one named last changes fastest.
Arguments:
- inverse_first: float32 [2, 512, 512], P(None, 'rows'), may hold values from -1.5 to 1.5, as said below
- inverse_second: float32 [2, 512, 512], P(None, 'rows'), may hold values from -1.5 to 1.5, as said below
- coupling: float32 [2, 512, 512], P(None, None, 'rows'), may hold values from -0.1875 to 0.1875
- head_rhs: float32 [2, 1024, 1024], P(None, None, 'wide'), may hold values from -6 to 6
- panel_rows: bfloat16 [131072, 2048], P(('rows', 'wide')), may hold values from -0.125 to 0.125
- trail_rhs: float32 [2, 131072, 1024], P(None, ('rows', 'wide')), may hold values from -6 to 6
Outputs:
- solved_first: float32 [2, 512, 1024], P(None, 'rows', 'wide')
- solved_second: float32 [2, 512, 1024], P(None, 'rows', 'wide')
- trail_updated: float32 [2, 131072, 1024], P(None, ('rows', 'wide'))
The draws below stay inside these ranges and needn't reach their ends.
Inputs may be any that keep to these rules, and one draw needn't show every extreme that they name: `inverse_first`: lower triangular in both planes: every entry above the diagonal is zero. `inverse_second`: lower triangular in both planes: every entry above the diagonal is zero.
All inputs are finite; a program needn't handle non-finite values.
Results may differ from the reference program's by a relative error of at most 0.0025.
Values may be sent and summed in bfloat16 or wider, within the bound.
A program may use at most 64 MiB of HBM per device.

```python
import math
import jax
import jax.numpy as jnp
from jax import lax

NB = 512
NRHS = 1024
TRAIL_DEV = 512
WIN = 1024
TRAIL_ROWS = 131072


def triangle_from(key, offdiag):
    keys = jax.random.split(key, 2)
    diag_real = jax.random.uniform(keys[0], (NB,), jnp.float32, 0.7, 1.4)
    diag_imag = jax.random.uniform(keys[1], (NB,), jnp.float32, -0.3, 0.3)
    row_index = jnp.arange(NB)[:, None]
    col_index = jnp.arange(NB)[None, :]
    strict = (row_index > col_index).astype(jnp.float32)
    onediag = (row_index == col_index).astype(jnp.float32)
    real_plane = offdiag[0] * strict + onediag * diag_real[None, :]
    imag_plane = offdiag[1] * strict + onediag * diag_imag[None, :]
    return jnp.stack([real_plane, imag_plane]).astype(jnp.float32)


def draw_inverse_first(key, part):
    key = jax.random.fold_in(key, 11)
    keys = jax.random.split(key, 2)
    scale_off = 0.6 / math.sqrt(NB)
    offdiag = jnp.clip(jax.random.normal(keys[0], (2, NB, NB), jnp.float32), -4.0, 4.0) * scale_off
    return triangle_from(keys[1], offdiag)


def draw_inverse_second(key, part):
    key = jax.random.fold_in(key, 23)
    keys = jax.random.split(key, 2)
    scale_off = 0.6 / math.sqrt(NB)
    offdiag = jnp.clip(jax.random.normal(keys[0], (2, NB, NB), jnp.float32), -4.0, 4.0) * scale_off
    return triangle_from(keys[1], offdiag)


def steps_of(stream_key, shape, cuts, least, high):
    loudness, own = 1.0, jax.random.fold_in(stream_key, 6)
    for axis_at, parts in cuts:
        draws = jnp.exp(jax.random.uniform(jax.random.fold_in(own, axis_at), (parts,), jnp.float32, least / len(cuts), high / len(cuts)))
        loudness = loudness * jnp.repeat(draws, shape[axis_at] // parts).reshape([-1 if axis == axis_at else 1 for axis in range(len(shape))])
    return loudness


def bell_draw(own_key, shape, scale, bound, shards=(), kind=jnp.bfloat16):
    level = steps_of(own_key, shape, shards, -0.22, 0.18) if shards else 1.0
    values = jax.random.normal(own_key, shape, jnp.float32) * scale * level
    return jnp.minimum(jnp.maximum(values, -bound), bound).astype(kind)


def setup_inputs(seed: int = 0) -> dict:
    key_of = jax.random.split(jax.random.key(seed), 7)
    return {
        "inverse_first": draw_inverse_first(jax.random.fold_in(key_of[6], 71), 0),
        "inverse_second": draw_inverse_second(jax.random.fold_in(key_of[6], 71), 0),
        "coupling": bell_draw(key_of[2], (2, NB, NB), (2 * NB) ** -0.5, 0.1875, ((2, 8),), jnp.float32),
        "head_rhs": bell_draw(key_of[3], (2, WIN, NRHS), 1.0, 6.0, ((2, 32),), jnp.float32),
        "panel_rows": bell_draw(key_of[4], (TRAIL_ROWS, 2 * WIN), (2 * WIN) ** -0.5, 0.125, ((0, 256),)),
        "trail_rhs": bell_draw(key_of[5], (2, TRAIL_ROWS, NRHS), 1.0, 6.0, ((1, 256),), jnp.float32),
    }


def complex_mul(left, right):
    highest = lax.Precision.HIGHEST
    real_part = jnp.dot(left[0], right[0], precision=highest, preferred_element_type=jnp.float32) - jnp.dot(left[1], right[1], precision=highest, preferred_element_type=jnp.float32)
    imag_part = jnp.dot(left[0], right[1], precision=highest, preferred_element_type=jnp.float32) + jnp.dot(left[1], right[0], precision=highest, preferred_element_type=jnp.float32)
    return jnp.stack([real_part, imag_part])


def reference(inverse_first, inverse_second, coupling, head_rhs, panel_rows, trail_rhs):
    solved_first = complex_mul(inverse_first, head_rhs[:, :NB])
    coupled = complex_mul(coupling, solved_first)
    solved_second = complex_mul(inverse_second, head_rhs[:, NB:] - coupled)
    solved_low = jnp.stack([solved_first, solved_second], 1).astype(jnp.bfloat16)
    real_low = solved_low[0].reshape(WIN, NRHS).astype(jnp.float32)
    imag_low = solved_low[1].reshape(WIN, NRHS).astype(jnp.float32)
    right_real = jnp.concatenate([real_low, -imag_low], 0)
    right_imag = jnp.concatenate([imag_low, real_low], 0)
    blocks = TRAIL_ROWS // TRAIL_DEV
    panel_blocks = panel_rows.reshape(blocks, TRAIL_DEV, 2 * WIN)
    rhs_blocks = jnp.transpose(trail_rhs.reshape(2, blocks, TRAIL_DEV, NRHS), (1, 0, 2, 3))

    def one_block(pair):
        panel_part, rhs_part = pair
        wide_panel = panel_part.astype(jnp.float32)
        real_part = jnp.dot(wide_panel, right_real, preferred_element_type=jnp.float32)
        imag_part = jnp.dot(wide_panel, right_imag, preferred_element_type=jnp.float32)
        return rhs_part - jnp.stack([real_part, imag_part])

    updated = lax.map(one_block, (panel_blocks, rhs_blocks))
    trail_updated = jnp.transpose(updated, (1, 0, 2, 3)).reshape(2, TRAIL_ROWS, NRHS)
    return solved_first, solved_second, trail_updated
```

```python
import functools

import jax
import jax.numpy as jnp
from jax import lax
from jax.experimental import pallas as pl
from jax.experimental.pallas import tpu as pltpu
from jax.sharding import PartitionSpec as P

MESH = pl.DeviceIdType.MESH
F32 = jnp.float32
BF16 = jnp.bfloat16
NX, NY, NZ = 4, 4, 8
NT = (((1,), (1,)), ((), ()))
NN = (((1,), (0,)), ((), ()))


def split(value):
    high = value.astype(BF16)
    return high, (value - high.astype(F32)).astype(BF16)


def dot3(left, right, dims):
    left_high, left_low = split(left)
    right_high, right_low = split(right)
    dot = functools.partial(lax.dot_general, dimension_numbers=dims, preferred_element_type=F32)
    return dot(left_high, right_high) + (dot(left_low, right_high) + dot(left_high, right_low))


def swap(value):
    return pltpu.roll(value, 64, 1)


def first_lanes(shape):
    return lax.broadcasted_iota(jnp.int32, shape, 1) < 64


def solve(rhs, inverse):
    both = dot3(rhs, inverse, NT)
    top, low = both[:32], swap(both[32:])
    return jnp.where(first_lanes(top.shape), top - low, top + low)


class Net:
    def __init__(self, gathered, sems):
        self.g = gathered
        self.sems = sems
        self.rows = lax.axis_index("rows")
        self.wide = lax.axis_index("wide")
        self.x, self.core = lax.div(self.rows, 2), lax.rem(self.rows, 2)
        self.z, self.y = lax.div(self.wide, NY), lax.rem(self.wide, NY)

    def at_x(self, step):
        return lax.rem(self.x + (step + NX), NX)

    def at_y(self, step):
        return lax.rem(self.y + (step + NY), NY)

    def at_z(self, step):
        return lax.rem(self.z + (step + NZ), NZ)

    def copy(self, ref, kind, half, index, rows, wide):
        send, recv = self.sems[kind]
        return pltpu.make_async_remote_copy(
            src_ref=ref,
            dst_ref=ref,
            send_sem=send.at[half, index],
            recv_sem=recv.at[half, index],
            device_id=(rows, wide),
            device_id_type=MESH,
        )

    def own(self):
        return self.z, pl.ds(pl.multiple_of(self.y * 32, 32), 32)

    def sibling(self):
        return self.rows + 1 - 2 * self.core

    def to_sibling(self, ref, half, index):
        return self.copy(ref, "sib", half, index, self.sibling(), self.wide)


class Even(Net):
    def first(self, half, back=False):
        z, cols = self.own()
        out = []
        for j in range(1, NX):
            at = self.at_x(-j) if back else self.x
            ref = self.g.at[half, 0, at, z, cols]
            out.append(self.copy(ref, "one", half, j, 2 * self.at_x(j), self.wide))
        return out

    def second(self, half, back=False):
        out = []
        for j in range(1, NY):
            y = self.at_y(-j) if back else self.y
            ref = self.g.at[half, 0, :, self.z, pl.ds(pl.multiple_of(y * 32, 32), 32)]
            out.append(self.copy(ref, "two", half, j, self.rows, self.z * NY + self.at_y(j)))
        return out

    def ring(self, half, way, step, chunk, back=False):
        z = self.at_z(-way * (step if back else step - 1))
        ref = self.g.at[half, 0, pl.ds(2 * chunk, 2), z]
        index = (0 if way == 1 else 8) + (step - 1) * 2 + chunk
        return self.copy(ref, "ring", half, index, self.rows, self.at_z(way) * NY + self.y)

    def hops(self, step):
        if step == 4:
            return [(1, 0), (-1, 1)]
        return [(1, 0), (-1, 1), (1, 1), (-1, 0)]

    steps = 4

    def sib(self, half, step):
        moves = {0: [(0, 0)], 4: [(4, 4)]}.get(step, [(step, -step), (step + 4, step)])
        return [
            self.to_sibling(self.g.at[half, 0, :, self.at_z(move)], half, index)
            for index, move in moves
        ]


class Odd(Net):
    def first(self, half, back=False):
        cols = self.own()[1]
        out = []
        for j in range(1, NZ):
            z = self.at_z(-j) if back else self.z
            ref = self.g.at[half, 1, self.x, z, cols]
            out.append(self.copy(ref, "one", half, j, self.rows, self.at_z(j) * NY + self.y))
        return out

    def second(self, half, back=False):
        out = []
        for j in range(1, NY):
            y = self.at_y(-j) if back else self.y
            ref = self.g.at[half, 1, self.x, :, pl.ds(pl.multiple_of(y * 32, 32), 32)]
            out.append(self.copy(ref, "two", half, j, self.rows, self.z * NY + self.at_y(j)))
        return out

    def ring(self, half, way, step, chunk, back=False):
        x = self.at_x(-way * (step if back else step - 1))
        ref = self.g.at[half, 1, x, pl.ds(2 * chunk, 2)]
        index = (0 if way == 1 else 8) + (step - 1) * 4 + chunk
        return self.copy(ref, "ring", half, index, 2 * self.at_x(way) + 1, self.wide)

    def hops(self, step):
        if step == 2:
            return [(1, 0), (-1, 2), (1, 1), (-1, 3)]
        return [(1, 0), (-1, 2), (1, 1), (-1, 3), (1, 2), (-1, 0), (1, 3), (-1, 1)]

    steps = 2

    def sib(self, half, step):
        moves = {0: [(0, 0)], 1: [(1, -1), (2, 1)], 2: [(3, 2)]}[step]
        return [
            self.to_sibling(self.g.at[half, 1, self.at_x(move)], half, index)
            for index, move in moves
        ]


def kernel(
    inv1_hbm, inv2_hbm, coup_hbm, head_hbm, panel_hbm, trail_hbm,
    out1, out2, acc,
    inv1, inv2, coup, head, panel, lhs, gathered, parts, sums, whole,
    local, rs_send, rs_recv, ag_send, ag_recv,
    one_send, one_recv, two_send, two_recv, ring_send, ring_recv, sib_send, sib_recv,
):
    loads = [
        pltpu.make_async_copy(src, dst, local.at[i])
        for i, (src, dst) in enumerate(
            [
                (head_hbm, head),
                (inv1_hbm, inv1),
                (coup_hbm, coup),
                (inv2_hbm, inv2),
                (panel_hbm, panel),
                (trail_hbm, acc),
            ]
        )
    ]
    for load in loads:
        load.start()

    sems = {
        "one": (one_send, one_recv),
        "two": (two_send, two_recv),
        "ring": (ring_send, ring_recv),
        "sib": (sib_send, sib_recv),
    }
    nets = Even(gathered, sems), Odd(gathered, sems)
    me = nets[0]
    rows, wide, x, core = me.rows, me.wide, me.x, me.core

    def by_core(step):
        for at, net in enumerate(nets):
            pl.when(core == at)(functools.partial(step, net))

    barrier = pltpu.get_barrier_semaphore()

    def greet(rows_at, wide_at):
        pl.semaphore_signal(barrier, inc=1, device_id=(rows_at, wide_at), device_id_type=MESH)

    def enter(net):
        for j in range(1, 2 * NX):
            greet(lax.rem(rows + j, 2 * NX), wide)
        for j in range(1, NY):
            greet(rows, me.z * NY + me.at_y(j))
        z_steps = (1, -1) if net is nets[0] else range(1, NZ)
        for j in z_steps:
            greet(rows, me.at_z(j) * NY + me.y)

    by_core(enter)

    loads[0].wait()
    loads[1].wait()
    solved = solve(head[:, :512], inv1[...])
    own_z, own_cols = me.own()
    gathered[0, core, x, own_z, own_cols, :] = solved.astype(BF16)
    first = first_lanes(solved.shape)
    turned = swap(solved)
    out1[0] = solved[:, :64]
    out1[1] = turned[:, :64]
    loads[2].wait()
    left = jnp.concatenate([jnp.where(first, solved, -solved), turned], 0)
    parts[...] = dot3(left, coup[...], NN).reshape(parts.shape)

    by_core(
        lambda net: pl.semaphore_wait(barrier, 2 * NX - 1 + NY - 1 + (2 if net is nets[0] else NZ - 1))
    )

    def peer(j):
        return lax.rem(rows + j, 2 * NX)

    def reduce_copy(j):
        return pltpu.make_async_remote_copy(
            src_ref=parts.at[peer(j)],
            dst_ref=sums.at[j],
            send_sem=rs_send.at[j],
            recv_sem=rs_recv.at[j],
            device_id=(peer(j), wide),
            device_id_type=MESH,
        )

    def share_copy(j, back=False):
        ref = whole.at[peer(2 * NX - j) if back else rows]
        return pltpu.make_async_remote_copy(
            src_ref=ref,
            dst_ref=ref,
            send_sem=ag_send.at[j],
            recv_sem=ag_recv.at[j],
            device_id=(peer(j), wide),
            device_id_type=MESH,
        )

    def start(copies):
        for copy in copies:
            copy.start()

    def arrive(copies):
        for copy in copies:
            copy.wait_recv()

    order = (4, 3, 5, 2, 6, 1, 7)
    for j in order:
        reduce_copy(j).start()
    by_core(lambda net: start(net.first(0)))

    loads[4].wait()
    for half in range(2):
        for at in range(NX):
            base = 512 * half + 128 * at
            real = panel[:, base : base + 128].astype(F32)
            imag = panel[:, 1024 + base : 1024 + base + 128].astype(F32)
            head_lanes = first_lanes(real.shape)
            real_turned, imag_turned = swap(real), swap(imag)
            for c in range(2):
                k = (4 * c + at) * 128
                if c == 0:
                    plane0 = jnp.where(head_lanes, -real, imag_turned)
                    plane1 = jnp.where(head_lanes, -imag, -real_turned)
                else:
                    plane0 = jnp.where(head_lanes, -real_turned, imag)
                    plane1 = jnp.where(head_lanes, -imag_turned, -real)
                lhs[half, 0, :, k : k + 128] = plane0.astype(BF16)
                lhs[half, 1, :, k : k + 128] = plane1.astype(BF16)

    for j in order:
        reduce_copy(j).wait_recv()
    total = parts[rows]
    for j in range(1, 2 * NX):
        total += sums[j]
    whole[rows] = head[pl.ds(pl.multiple_of(8 * rows, 8), 8), 512:] - total
    for j in order:
        share_copy(j).start()

    def step_two(net, half):
        arrive(net.first(half, back=True))
        start(net.second(half))

    def ring_open(net, half):
        arrive(net.second(half, back=True))
        start(net.ring(half, way, 1, chunk) for way, chunk in net.hops(1))
        start(net.sib(half, 0))

    def ring_step(net, half, step):
        following = net.hops(step + 1) if step < net.steps else []
        for way, chunk in net.hops(step):
            net.ring(half, way, step, chunk, back=True).wait_recv()
            if (way, chunk) in following:
                net.ring(half, way, step + 1, chunk).start()
        start(net.sib(half, step))

    def ring_rest(net, half):
        for step in range(1, net.steps + 1):
            ring_step(net, half, step)

    by_core(lambda net: step_two(net, 0))

    for j in order:
        share_copy(j, back=True).wait_recv()
    loads[3].wait()
    solved = solve(whole[...].reshape(64, 512), inv2[...])
    gathered[1, core, x, own_z, own_cols, :] = solved.astype(BF16)
    by_core(lambda net: start(net.first(1)))
    by_core(lambda net: ring_open(net, 0))
    out2[0] = solved[:, :64]
    out2[1] = swap(solved)[:, :64]
    by_core(lambda net: step_two(net, 1))
    by_core(lambda net: ring_step(net, 0, 1))
    by_core(lambda net: ring_open(net, 1))

    def rest(net):
        for step in range(2, net.steps + 1):
            ring_step(net, 0, step)
        ring_rest(net, 1)

    by_core(rest)

    def from_sibling(net, half):
        other = nets[1] if net is nets[0] else nets[0]
        for step in range(other.steps + 1):
            arrive(other.sib(half, step))

    by_core(lambda net: from_sibling(net, 0))
    by_core(lambda net: from_sibling(net, 1))
    loads[5].wait()

    def product(n, carry):
        cols = pl.ds(pl.multiple_of(n * 256, 256), 256)
        for plane in range(2):
            total = acc[plane, :, cols]
            for half in range(2):
                right = jnp.concatenate(
                    [
                        gathered[half, c, at, pl.ds(2 * n, 2)].reshape(256, 128)
                        for c in range(2)
                        for at in range(NX)
                    ],
                    1,
                )
                total += lax.dot_general(lhs[half, plane], right, NT, preferred_element_type=F32)
            acc[plane, :, cols] = total
        return carry

    lax.fori_loop(0, 4, product, 0)

    for j in order:
        reduce_copy(j).wait_send()
        share_copy(j).wait_send()

    def leave(net):
        for half in range(2):
            for copy in net.first(half) + net.second(half):
                copy.wait_send()
            for step in range(1, net.steps + 1):
                for way, chunk in net.hops(step):
                    net.ring(half, way, step, chunk).wait_send()
            for step in range(net.steps + 1):
                for copy in net.sib(half, step):
                    copy.wait_send()

    by_core(leave)


def body(inverse_first, inverse_second, coupling, head_rhs, panel_rows, trail_rhs):
    dma = pltpu.SemaphoreType.DMA
    first, second, updated = pl.pallas_call(
        kernel,
        out_shape=(
            pltpu.VMEM((2, 32, 64), F32),
            pltpu.VMEM((2, 32, 64), F32),
            pltpu.VMEM((2, 512, 1024), F32),
        ),
        in_specs=[pl.BlockSpec(memory_space=pl.ANY)] * 6,
        out_specs=[pl.BlockSpec(memory_space=pltpu.VMEM)] * 3,
        scratch_shapes=[
            pltpu.VMEM((128, 512), F32),
            pltpu.VMEM((128, 512), F32),
            pltpu.VMEM((128, 512), F32),
            pltpu.VMEM((64, 1024), F32),
            pltpu.VMEM((512, 2048), BF16),
            pltpu.VMEM((2, 2, 512, 1024), BF16),
            pltpu.VMEM((2, 2, NX, NZ, 128, 128), BF16),
            pltpu.VMEM((8, 8, 512), F32),
            pltpu.VMEM((8, 8, 512), F32),
            pltpu.VMEM((8, 8, 512), F32),
            dma((6,)),
            dma((8,)),
            dma((8,)),
            dma((8,)),
            dma((8,)),
            dma((2, 8)),
            dma((2, 8)),
            dma((2, 4)),
            dma((2, 4)),
            dma((2, 16)),
            dma((2, 16)),
            dma((2, 8)),
            dma((2, 8)),
        ],
        compiler_params=pltpu.CompilerParams(
            collective_id=0, has_side_effects=True, vmem_limit_bytes=40 << 20
        ),
        cost_estimate=pl.CostEstimate(flops=4 << 30, bytes_accessed=12 << 20, transcendentals=0),
    )(
        inverse_first.reshape(128, 512),
        inverse_second.reshape(128, 512),
        jnp.transpose(coupling, (0, 2, 1)).reshape(128, 512),
        jnp.transpose(head_rhs, (0, 2, 1)).reshape(64, 1024),
        panel_rows,
        trail_rhs,
    )
    return jnp.transpose(first, (0, 2, 1)), jnp.transpose(second, (0, 2, 1)), updated


def solution(mesh):
    return jax.shard_map(
        body,
        mesh=mesh,
        in_specs=(
            P(None, "rows", None),
            P(None, "rows", None),
            P(None, None, "rows"),
            P(None, None, "wide"),
            P(("rows", "wide"), None),
            P(None, ("rows", "wide"), None),
        ),
        out_specs=(
            P(None, "rows", "wide"),
            P(None, "rows", "wide"),
            P(None, ("rows", "wide"), None),
        ),
        check_vma=False,
    )
```

```python
import functools

import jax
import jax.numpy as jnp
from jax import lax
from jax.experimental import pallas as pl
from jax.experimental.pallas import tpu as pltpu
from jax.sharding import PartitionSpec as P

MESH = pl.DeviceIdType.MESH
F32 = jnp.float32
BF16 = jnp.bfloat16
NX, NY, NZ = 4, 4, 8
NEAR = ((2, 2), (2, 1))
PLANE = sorted(
    ((i, j) for i in range(NX) for j in range(NY) if i or j),
    key=lambda p: -(min(p[0], NX - p[0]) + min(p[1], NY - p[1])),
)
NT = (((1,), (1,)), ((), ()))
NN = (((1,), (0,)), ((), ()))


def split(value):
    high = value.astype(BF16)
    return high, (value - high.astype(F32)).astype(BF16)


def dot3(left, right, dims):
    left_high, left_low = split(left)
    right_high, right_low = split(right)
    dot = functools.partial(lax.dot_general, dimension_numbers=dims, preferred_element_type=F32)
    return dot(left_high, right_high) + (dot(left_low, right_high) + dot(left_high, right_low))


def swap(value):
    return pltpu.roll(value, 64, 1)


def first_lanes(shape):
    return lax.broadcasted_iota(jnp.int32, shape, 1) < 64


def solve(rhs, inverse):
    both = dot3(rhs, inverse, NT)
    top, low = both[:32], swap(both[32:])
    return jnp.where(first_lanes(top.shape), top - low, top + low)


class Net:
    def __init__(self, gathered, sems):
        self.g, self.sems = gathered, sems
        self.rows, self.wide = lax.axis_index("rows"), lax.axis_index("wide")
        self.x, self.core = lax.div(self.rows, 2), lax.rem(self.rows, 2)
        self.z, self.y = lax.div(self.wide, NY), lax.rem(self.wide, NY)

    def on_rows(self, j):
        return lax.rem(self.rows + j, 2 * NX), self.wide

    def on_plane(self, i, j):
        x, y = lax.rem(self.x + i, NX), lax.rem(self.y + j, NY)
        return 2 * x + self.core, self.z * NY + y

    def on_z(self, j):
        return self.rows, lax.rem(self.z + j, NZ) * NY + self.y

    def sibling(self):
        return self.rows + 1 - 2 * self.core, self.wide

    def copy(self, src, dst, kind, half, index, to):
        send, recv = self.sems[kind]
        return pltpu.make_async_remote_copy(
            src_ref=src,
            dst_ref=dst,
            send_sem=send.at[half, index],
            recv_sem=recv.at[half, index],
            device_id=to,
            device_id_type=MESH,
        )

    def block(self, half, dz, i=0, j=0, core=None):
        x, y = lax.rem(self.x + (NX - i), NX), lax.rem(self.y + (NY - j), NY)
        return self.g.at[half, self.core if core is None else core, dz, y, x]

    def slab(self, half, dz, core=None):
        return self.g.at[half, self.core if core is None else core, dz]

    def far(self, half, near, i=0, j=0, core=None):
        return self.block(half, pl.ds(near + 1, NZ - 1 - 2 * near), i, j, core)

    def along_z(self, half, j):
        return self.copy(self.block(half, 0), self.block(half, NZ - j), "z", half, j, self.on_z(j))

    def over_plane(self, half, i, j, back=False):
        ref = self.block(half, 0, i, j) if back else self.block(half, 0)
        return self.copy(ref, ref, "p", half, NY * i + j, self.on_plane(i, j))

    def slab_along_z(self, half, j):
        return self.copy(self.slab(half, 0), self.slab(half, NZ - j), "b", half, j, self.on_z(j))

    def far_over(self, half, near, i, j, back=False):
        ref = self.far(half, near, i, j) if back else self.far(half, near)
        return self.copy(ref, ref, "f", half, NY * i + j, self.on_plane(i, j))

    def pass_slab(self, half, dz, back=False):
        ref = self.slab(half, dz, 1 - self.core if back else None)
        return self.copy(ref, ref, "s", half, 16 + dz, self.sibling())

    def pass_far(self, half, near, i, j, back=False):
        ref = self.far(half, near, i, j, 1 - self.core if back else None)
        return self.copy(ref, ref, "s", half, NY * i + j, self.sibling())


    def open(self, half, near):
        for j in far_steps(near):
            self.along_z(half, j).start()
        for i, j in PLANE:
            self.over_plane(half, i, j).start()

    def spread_plane(self, half, near):
        for i, j in PLANE[::-1]:
            self.over_plane(half, i, j, back=True).wait_recv()
        for j in near_steps(near):
            self.slab_along_z(half, j).start()
        self.pass_slab(half, 0).start()

    def spread_z(self, half, near):
        for j in far_steps(near)[::-1]:
            self.along_z(half, j).wait_recv()
        for i, j in PLANE:
            self.far_over(half, near, i, j).start()
        self.pass_far(half, near, 0, 0).start()

    def take_slabs(self, half, near):
        for j in near_steps(near):
            self.slab_along_z(half, j).wait_recv()
            self.pass_slab(half, NZ - j).start()

    def take_far(self, half, near):
        for i, j in PLANE[::-1]:
            self.far_over(half, near, i, j, back=True).wait_recv()
            self.pass_far(half, near, i, j).start()

    def finish(self, half, near):
        for dz in [0] + near_steps(near):
            self.pass_slab(half, dz, back=True).wait_recv()
        for i, j in [(0, 0)] + PLANE[::-1]:
            self.pass_far(half, near, i, j, back=True).wait_recv()

    def leave(self, half, near):
        for j in far_steps(near):
            self.along_z(half, j).wait_send()
        for i, j in PLANE:
            self.over_plane(half, i, j).wait_send()
            self.far_over(half, near, i, j).wait_send()
            self.pass_far(half, near, i, j).wait_send()
        self.pass_far(half, near, 0, 0).wait_send()
        for j in near_steps(near):
            self.slab_along_z(half, j).wait_send()
        for dz in [0] + near_steps(near):
            self.pass_slab(half, dz).wait_send()


def far_steps(near):
    return sorted(range(near + 1, NZ - near), key=lambda j: -min(j, NZ - j))


def near_steps(near):
    return [j for step in range(1, near + 1) for j in (step, NZ - step)]


def update(acc, lhs, gathered, half, plane, steps, columns):
    right = jnp.concatenate(
        [
            jnp.concatenate([gathered[half, c, dz, :, x].reshape(128, 128) for dz in steps], 0)
            for c in range(2)
            for x in range(NX)
        ],
        1,
    )
    product = lax.dot_general(lhs[half, plane], right, NT, preferred_element_type=F32)
    return [
        acc[plane, :, cols] + product[:, 128 * at : 128 * (at + 1)]
        for at, cols in enumerate(columns)
    ]


def columns_of(z, steps):
    return [pl.ds(pl.multiple_of(128 * lax.rem(z + dz, NZ), 128), 128) for dz in steps]


PAIRS = ((0, 1), (7, 2), (6, 3), (5, 4))


def gather_kernel(
    inv1_hbm, inv2_hbm, coup_hbm, head_hbm, panel_hbm, trail_hbm,
    out1, out2, acc, lhs, gathered,
    inv1, inv2, coup, head, panel, parts, sums, whole,
    local, rs_send, rs_recv, ag_send, ag_recv,
    z_send, z_recv, p_send, p_recv, b_send, b_recv, f_send, f_recv, s_send, s_recv,
):
    loads = [
        pltpu.make_async_copy(src, dst, local.at[i])
        for i, (src, dst) in enumerate(
            [
                (head_hbm, head),
                (inv1_hbm, inv1),
                (coup_hbm, coup),
                (inv2_hbm, inv2),
                (panel_hbm, panel),
                (trail_hbm, acc),
            ]
        )
    ]
    for load in loads:
        load.start()

    net = Net(
        gathered,
        {
            "z": (z_send, z_recv),
            "p": (p_send, p_recv),
            "b": (b_send, b_recv),
            "f": (f_send, f_recv),
            "s": (s_send, s_recv),
        },
    )
    rows, x, core = net.rows, net.x, net.core

    def stage(step, half, other=False):
        near = NEAR[half][::-1] if other else NEAR[half]
        if near[0] == near[1]:
            step(half, near[0])
        else:
            for at in range(2):
                pl.when(core == at)(functools.partial(step, half, near[at]))

    barrier = pltpu.get_barrier_semaphore()
    peers = [net.on_z(j) for j in far_steps(0)]
    peers += [net.on_plane(i, j) for i, j in PLANE if j]
    peers += [net.on_rows(j) for j in range(1, 2 * NX)]
    for peer in peers:
        pl.semaphore_signal(barrier, inc=1, device_id=peer, device_id_type=MESH)

    loads[0].wait()
    loads[1].wait()
    solved = solve(head[:, :512], inv1[...])
    gathered[0, core, 0, net.y, x] = solved.astype(BF16)
    first = first_lanes(solved.shape)
    turned = swap(solved)
    out1[0] = solved[:, :64]
    out1[1] = turned[:, :64]
    loads[2].wait()
    left = jnp.concatenate([jnp.where(first, solved, -solved), turned], 0)
    parts[...] = dot3(left, coup[...], NN).reshape(parts.shape)

    pl.semaphore_wait(barrier, len(peers))

    def reduce_copy(j):
        to = net.on_rows(j)
        return pltpu.make_async_remote_copy(
            src_ref=parts.at[to[0]],
            dst_ref=sums.at[j],
            send_sem=rs_send.at[j],
            recv_sem=rs_recv.at[j],
            device_id=to,
            device_id_type=MESH,
        )

    def share_copy(j, back=False):
        ref = whole.at[lax.rem(rows + (2 * NX - j), 2 * NX) if back else rows]
        return pltpu.make_async_remote_copy(
            src_ref=ref,
            dst_ref=ref,
            send_sem=ag_send.at[j],
            recv_sem=ag_recv.at[j],
            device_id=net.on_rows(j),
            device_id_type=MESH,
        )

    order = (4, 3, 5, 2, 6, 1, 7)
    for j in order:
        reduce_copy(j).start()
    stage(net.open, 0)

    loads[4].wait()
    for half in range(2):
        for at in range(NX):
            base = 512 * half + 128 * at
            real = panel[:, base : base + 128].astype(F32)
            imag = panel[:, 1024 + base : 1024 + base + 128].astype(F32)
            head_lanes = first_lanes(real.shape)
            real_turned, imag_turned = swap(real), swap(imag)
            for c in range(2):
                k = (NX * c + at) * 128
                if c == 0:
                    plane0 = jnp.where(head_lanes, -real, imag_turned)
                    plane1 = jnp.where(head_lanes, -imag, -real_turned)
                else:
                    plane0 = jnp.where(head_lanes, -real_turned, imag)
                    plane1 = jnp.where(head_lanes, -imag_turned, -real)
                lhs[half, 0, :, k : k + 128] = plane0.astype(BF16)
                lhs[half, 1, :, k : k + 128] = plane1.astype(BF16)

    for j in order:
        reduce_copy(j).wait_recv()
    total = parts[rows]
    for j in range(1, 2 * NX):
        total += sums[j]
    whole[rows] = head[pl.ds(pl.multiple_of(8 * rows, 8), 8), 512:] - total
    for j in order:
        share_copy(j).start()

    stage(net.spread_plane, 0)
    for j in order:
        share_copy(j, back=True).wait_recv()
    loads[3].wait()
    solved = solve(whole[...].reshape(64, 512), inv2[...])
    gathered[1, core, 0, net.y, x] = solved.astype(BF16)
    stage(net.open, 1)
    out2[0] = solved[:, :64]
    out2[1] = swap(solved)[:, :64]

    stage(net.spread_z, 0)
    stage(net.take_slabs, 0)
    stage(net.spread_plane, 1)
    stage(net.spread_z, 1)
    stage(net.take_far, 0)
    stage(net.finish, 0, other=True)
    loads[5].wait()

    def product(at):
        columns = columns_of(net.z, PAIRS[at])
        for plane in range(2):
            for cols, value in zip(columns, update(acc, lhs, gathered, 0, plane, PAIRS[at], columns)):
                acc[plane, :, cols] = value

    product(0)
    product(1)
    stage(net.take_slabs, 1)
    product(2)
    product(3)
    stage(net.take_far, 1)
    stage(net.finish, 1, other=True)

    for j in order:
        reduce_copy(j).wait_send()
        share_copy(j).wait_send()
    stage(net.leave, 0)
    stage(net.leave, 1)


def write_kernel(first, second, acc, lhs, gathered, out1, out2, out, stage, sems):
    z = lax.div(lax.axis_index("wide"), NY)
    copies = [
        pltpu.make_async_copy(first, out1, sems.at[8]),
        pltpu.make_async_copy(second, out2, sems.at[9]),
    ]
    for copy in copies:
        copy.start()
    for at, steps in enumerate(PAIRS):
        columns = columns_of(z, steps)
        for plane in range(2):
            for cols, value in zip(columns, update(acc, lhs, gathered, 1, plane, steps, columns)):
                stage[plane, :, cols] = value
        for k, cols in enumerate(columns):
            copies.append(
                pltpu.make_async_copy(
                    stage.at[:, :, cols], out.at[:, :, cols], sems.at[2 * at + k]
                )
            )
            copies[-1].start()
    for copy in copies:
        copy.wait()


def body(inverse_first, inverse_second, coupling, head_rhs, panel_rows, trail_rhs):
    dma = pltpu.SemaphoreType.DMA
    pair = [dma((2, 16)), dma((2, 16))]
    held = pl.pallas_call(
        gather_kernel,
        out_shape=(
            pltpu.VMEM((2, 32, 64), F32),
            pltpu.VMEM((2, 32, 64), F32),
            pltpu.VMEM((2, 512, 1024), F32),
            pltpu.VMEM((2, 2, 512, 1024), BF16),
            pltpu.VMEM((2, 2, NZ, NY, NX, 32, 128), BF16),
        ),
        in_specs=[pl.BlockSpec(memory_space=pltpu.HBM)] * 6,
        out_specs=[pl.BlockSpec(memory_space=pltpu.VMEM)] * 5,
        scratch_shapes=[
            pltpu.VMEM((128, 512), F32),
            pltpu.VMEM((128, 512), F32),
            pltpu.VMEM((128, 512), F32),
            pltpu.VMEM((64, 1024), F32),
            pltpu.VMEM((512, 2048), BF16),
            pltpu.VMEM((8, 8, 512), F32),
            pltpu.VMEM((8, 8, 512), F32),
            pltpu.VMEM((8, 8, 512), F32),
            dma((6,)),
            dma((8,)),
            dma((8,)),
            dma((8,)),
            dma((8,)),
            *pair * 4,
            dma((2, 24)),
            dma((2, 24)),
        ],
        compiler_params=pltpu.CompilerParams(
            collective_id=0, has_side_effects=True, vmem_limit_bytes=24 << 20
        ),
        cost_estimate=pl.CostEstimate(flops=2 << 30, bytes_accessed=8 << 20, transcendentals=0),
    )(
        *(
            pltpu.with_memory_space_constraint(operand, pltpu.HBM)
            for operand in (
                inverse_first.reshape(128, 512),
                inverse_second.reshape(128, 512),
                jnp.transpose(coupling, (0, 2, 1)).reshape(128, 512),
                jnp.transpose(head_rhs, (0, 2, 1)).reshape(64, 1024),
                panel_rows,
                trail_rhs,
            )
        )
    )
    first, second, updated = pl.pallas_call(
        write_kernel,
        out_shape=(
            jax.ShapeDtypeStruct((2, 32, 64), F32),
            jax.ShapeDtypeStruct((2, 32, 64), F32),
            jax.ShapeDtypeStruct((2, 512, 1024), F32),
        ),
        in_specs=[pl.BlockSpec(memory_space=pltpu.VMEM)] * 5,
        out_specs=[pl.BlockSpec(memory_space=pltpu.HBM)] * 3,
        scratch_shapes=[pltpu.VMEM((2, 512, 1024), F32), dma((10,))],
        compiler_params=pltpu.CompilerParams(vmem_limit_bytes=16 << 20),
        cost_estimate=pl.CostEstimate(flops=2 << 30, bytes_accessed=4 << 20, transcendentals=0),
    )(*(pltpu.with_memory_space_constraint(value, pltpu.VMEM) for value in held))
    return jnp.transpose(first, (0, 2, 1)), jnp.transpose(second, (0, 2, 1)), updated


def solution(mesh):
    return jax.shard_map(
        body,
        mesh=mesh,
        in_specs=(
            P(None, "rows", None),
            P(None, "rows", None),
            P(None, None, "rows"),
            P(None, None, "wide"),
            P(("rows", "wide"), None),
            P(None, ("rows", "wide"), None),
        ),
        out_specs=(
            P(None, "rows", "wide"),
            P(None, "rows", "wide"),
            P(None, ("rows", "wide"), None),
        ),
        check_vma=False,
    )
```

```python
import functools

import jax
import jax.numpy as jnp
from jax import lax
from jax.experimental import pallas as pl
from jax.experimental.pallas import tpu as pltpu
from jax.sharding import PartitionSpec as P

MESH = pl.DeviceIdType.MESH
F32 = jnp.float32
BF16 = jnp.bfloat16
NX, NY, NZ = 4, 4, 8
NEAR = ((2, 2), (2, 1))
RELAY = (0,)
PLANE = sorted(
    ((i, j) for i in range(NX) for j in range(NY) if i or j),
    key=lambda p: -(min(p[0], NX - p[0]) + min(p[1], NY - p[1])),
)
GROUPS, BOXES = (PLANE[-4:], PLANE[3:-4], PLANE[:3]), ((4, 1), (4, 2), (3, 1))
SENT_FIRST, SENT, SENT_ON = range(3)
OVER_PLANE, ALONG_Z, NEAR_ON, REST_ON, SLABS, FAR = 0, 1, 2, 3, 3, 6
NT = (((1,), (1,)), ((), ()))
NN = (((1,), (0,)), ((), ()))


def split(value):
    high = value.astype(BF16)
    return high, (value - high.astype(F32)).astype(BF16)


def dot3(left, right, dims):
    (left_high, left_low), (right_high, right_low) = left, right
    dot = functools.partial(lax.dot_general, dimension_numbers=dims, preferred_element_type=F32)
    return dot(left_high, right_high) + (dot(left_low, right_high) + dot(left_high, right_low))


def swap(value):
    return pltpu.roll(value, 64, 1)


def first_lanes(shape):
    return lax.broadcasted_iota(jnp.int32, shape, 1) < 64


def solve(rhs, inverse):
    both = dot3(split(rhs), inverse, NT)
    top, low = both[:32], swap(both[32:])
    return jnp.where(first_lanes(top.shape), top - low, top + low)


class Net:
    def __init__(self, gathered, sems):
        self.g, self.sems = gathered, sems
        self.rows, self.wide = lax.axis_index("rows"), lax.axis_index("wide")
        self.x, self.core = lax.div(self.rows, 2), lax.rem(self.rows, 2)
        self.z, self.y = lax.div(self.wide, NY), lax.rem(self.wide, NY)

    def on_rows(self, j):
        return lax.rem(self.rows + j, 2 * NX), self.wide

    def on_plane(self, i, j):
        x, y = lax.rem(self.x + i, NX), lax.rem(self.y + j, NY)
        return 2 * x + self.core, self.z * NY + y

    def on_z(self, j):
        return self.rows, lax.rem(self.z + j, NZ) * NY + self.y

    def sibling(self):
        return self.rows + 1 - 2 * self.core, self.wide

    def copy(self, src, dst, half, sent, landed, to):
        send, recv = self.sems
        return pltpu.make_async_remote_copy(
            src_ref=src,
            dst_ref=dst,
            send_sem=send.at[half, sent],
            recv_sem=recv.at[half, landed],
            device_id=to,
            device_id_type=MESH,
        )

    def block(self, half, dz, i=0, j=0, core=None):
        x, y = lax.rem(self.x + (NX - i), NX), lax.rem(self.y + (NY - j), NY)
        return self.g.at[half, self.core if core is None else core, dz, y, x]

    def slab(self, half, dz):
        return self.g.at[half, self.core, dz]

    def far(self, half, near):
        return self.block(half, pl.ds(near + 1, NZ - 1 - 2 * near))

    def along_z(self, half, j):
        src, dst = self.block(half, 0), self.block(half, NZ - j)
        return self.copy(src, dst, half, SENT, ALONG_Z, self.on_z(j))

    def over_plane(self, half, i, j):
        ref = self.block(half, 0)
        return self.copy(ref, ref, half, SENT_FIRST, OVER_PLANE, self.on_plane(i, j))

    def slabs_along_z(self, half, step):
        for j in (step, NZ - step):
            src, dst = self.slab(half, 0), self.slab(half, NZ - j)
            yield self.copy(src, dst, half, SENT, SLABS + step, self.on_z(j))

    def far_over(self, half, near, i, j):
        ref = self.far(half, near)
        landed = FAR + next(at for at, group in enumerate(GROUPS) if (i, j) in group)
        return self.copy(ref, ref, half, SENT, landed, self.on_plane(i, j))

    def hand_on(self, half, ref, landed):
        self.copy(ref, ref, half, SENT_ON, landed, self.sibling()).start()

    def wait(self, half, blocks, sent=None, landed=None):
        z, y, x = blocks
        ref = self.g.at[half, self.core, pl.ds(0, z), pl.ds(0, y), pl.ds(0, x)]
        copy = self.copy(ref, ref, half, sent or 0, landed or 0, self.sibling())
        if landed is None:
            copy.wait_send()
        else:
            copy.wait_recv()


    def open(self, half, near):
        for j in far_steps(near):
            self.along_z(half, j).start()
        for i, j in PLANE:
            self.over_plane(half, i, j).start()

    def spread_plane(self, half, near):
        self.wait(half, (5, 3, 1), landed=OVER_PLANE)
        for step in range(1, (1 if half in RELAY else near) + 1):
            for copy in self.slabs_along_z(half, step):
                copy.start()
        self.hand_on(half, self.slab(half, 0), NEAR_ON)

    def relay(self, half, near):
        self.wait(half, (2, NY, NX), landed=SLABS + 1)
        for dz, way in ((NZ - 1, 1), (1, NZ - 1)):
            src, dst = self.slab(half, dz), self.slab(half, 2 * dz % NZ)
            self.copy(src, dst, half, SENT, SLABS + 2, self.on_z(way)).start()
        for dz in (1, NZ - 1):
            self.hand_on(half, self.slab(half, dz), NEAR_ON)

    def spread_z(self, half, near):
        self.wait(half, (NZ - 1 - 2 * near, 1, 1), landed=ALONG_Z)
        for i, j in [(2, 2), (1, 2), (3, 2), (0, 2), (2, 1), (1, 1), (3, 1), (0, 1), (2, 3), (1, 3), (3, 3), (0, 3), (2, 0), (1, 0), (3, 0)]:
            self.far_over(half, near, i, j).start()
        self.hand_on(half, self.far(half, near), REST_ON)

    def take_slabs(self, half, near):
        for step in range(2 if half in RELAY else 1, near + 1):
            self.wait(half, (2, NY, NX), landed=SLABS + step)
            for dz in (step, NZ - step):
                self.hand_on(half, self.slab(half, dz), NEAR_ON if step == 1 else REST_ON)

    def take_far(self, half, near, at):
        count = NZ - 1 - 2 * near
        self.wait(half, (count, *BOXES[at]), landed=FAR + at)
        for i, j in GROUPS[at]:
            self.hand_on(half, self.block(half, pl.ds(near + 1, count), i, j), REST_ON)

    def finish_near(self, half):
        self.wait(half, (3, NY, NX), landed=NEAR_ON)

    def finish_rest(self, half):
        self.wait(half, (NZ - 3, NY, NX), landed=REST_ON)

    def leave(self, half):
        self.wait(half, (5, 3, 1), sent=SENT_FIRST)
        self.wait(half, (NZ - 1, NY, NX), sent=SENT)
        self.wait(half, (NZ, NY, NX), sent=SENT_ON)


def far_steps(near):
    return sorted(range(near + 1, NZ - near), key=lambda j: -min(j, NZ - j))


def update(acc, lhs, gathered, half, plane, steps, columns):
    right = jnp.concatenate(
        [
            jnp.concatenate([gathered[half, c, dz, :, x].reshape(128, 128) for dz in steps], 0)
            for c in range(2)
            for x in range(NX)
        ],
        1,
    )
    product = lax.dot_general(lhs[half, plane], right, NT, preferred_element_type=F32)
    return [
        acc[plane, :, cols] + product[:, 128 * at : 128 * (at + 1)]
        for at, cols in enumerate(columns)
    ]


def columns_of(z, steps):
    return [pl.ds(pl.multiple_of(128 * lax.rem(z + dz, NZ), 128), 128) for dz in steps]


NEAR_STEPS, REST_STEPS = ((0, 1), (7,)), ((2, 3), (4, 5), (6,))


def gather_kernel(
    inv1_hbm, inv2_hbm, coup_hbm, head_hbm, panel_hbm, trail_hbm,
    out1, out2, acc, lhs, gathered,
    inv1, inv2, coup, head, panel, parts, sums, whole, inv2_split,
    local, sum_sems, send_sems, recv_sems,
):
    loads = [
        pltpu.make_async_copy(src, dst, local.at[i])
        for i, (src, dst) in enumerate(
            [
                (head_hbm, head),
                (inv1_hbm, inv1),
                (coup_hbm, coup),
                (inv2_hbm, inv2),
                (panel_hbm, panel),
                (trail_hbm, acc),
            ]
        )
    ]
    for load in loads[:3]:
        load.start()

    net = Net(gathered, (send_sems, recv_sems))
    rows, x, core = net.rows, net.x, net.core

    def stage(step, half, *more):
        near = NEAR[half]
        if near[0] == near[1]:
            step(half, near[0], *more)
        else:
            for at in range(2):
                pl.when(core == at)(functools.partial(step, half, near[at], *more))

    barrier = pltpu.get_barrier_semaphore()
    peers = [net.on_z(j) for j in far_steps(0)]
    peers += [net.on_plane(i, j) for i, j in PLANE if j]
    peers += [net.on_rows(j) for j in range(1, 2 * NX)]
    for peer in peers:
        pl.semaphore_signal(barrier, inc=1, device_id=peer, device_id_type=MESH)

    loads[0].wait()
    loads[1].wait()
    for load in loads[3:]:
        load.start()
    solved = solve(head[:, :512], split(inv1[...]))
    gathered[0, core, 0, net.y, x] = solved.astype(BF16)
    first = first_lanes(solved.shape)
    turned = swap(solved)
    out1[0] = solved[:, :64]
    out1[1] = turned[:, :64]
    loads[2].wait()
    left = jnp.concatenate([jnp.where(first, solved, -solved), turned], 0)
    parts[...] = dot3(split(left), split(coup[...]), NN).reshape(parts.shape)

    pl.semaphore_wait(barrier, len(peers))

    def reduce_copy(j):
        to = net.on_rows(j)
        return pltpu.make_async_remote_copy(
            src_ref=parts.at[to[0]],
            dst_ref=sums.at[j],
            send_sem=sum_sems.at[0],
            recv_sem=sum_sems.at[1],
            device_id=to,
            device_id_type=MESH,
        )

    def share_copy(j):
        ref = whole.at[rows]
        return pltpu.make_async_remote_copy(
            src_ref=ref,
            dst_ref=ref,
            send_sem=sum_sems.at[2],
            recv_sem=sum_sems.at[3],
            device_id=net.on_rows(j),
            device_id_type=MESH,
        )

    def all_seven(ref, at):
        ref = ref.at[pl.ds(1, 2 * NX - 1)]
        return pltpu.make_async_remote_copy(
            src_ref=ref,
            dst_ref=ref,
            send_sem=sum_sems.at[at],
            recv_sem=sum_sems.at[at + 1],
            device_id=net.sibling(),
            device_id_type=MESH,
        )

    order = (4, 3, 5, 2, 6, 1, 7)
    for j in order:
        reduce_copy(j).start()
    stage(net.open, 0)

    loads[4].wait()
    for half in range(2):
        for at in range(NX):
            base = 512 * half + 128 * at
            real = panel[:, base : base + 128].astype(F32)
            imag = panel[:, 1024 + base : 1024 + base + 128].astype(F32)
            head_lanes = first_lanes(real.shape)
            real_turned, imag_turned = swap(real), swap(imag)
            for c in range(2):
                k = (NX * c + at) * 128
                if c == 0:
                    plane0 = jnp.where(head_lanes, -real, imag_turned)
                    plane1 = jnp.where(head_lanes, -imag, -real_turned)
                else:
                    plane0 = jnp.where(head_lanes, -real_turned, imag)
                    plane1 = jnp.where(head_lanes, -imag_turned, -real)
                lhs[half, 0, :, k : k + 128] = plane0.astype(BF16)
                lhs[half, 1, :, k : k + 128] = plane1.astype(BF16)

    loads[3].wait()
    inv2_split[0], inv2_split[1] = split(inv2[...])

    all_seven(sums, 0).wait_recv()
    total = parts[rows]
    for j in range(1, 2 * NX):
        total += sums[j]
    whole[rows] = head[pl.ds(pl.multiple_of(8 * rows, 8), 8), 512:] - total
    for j in order:
        share_copy(j).start()

    stage(net.spread_plane, 0)
    stage(net.spread_z, 0)
    all_seven(whole, 2).wait_recv()
    solved = solve(whole[...].reshape(64, 512), (inv2_split[0], inv2_split[1]))
    gathered[1, core, 0, net.y, x] = solved.astype(BF16)
    stage(net.open, 1)
    out2[0] = solved[:, :64]
    out2[1] = swap(solved)[:, :64]

    def product(half, steps):
        columns = columns_of(net.z, steps)
        for plane in range(2):
            for cols, value in zip(columns, update(acc, lhs, gathered, half, plane, steps, columns)):
                acc[plane, :, cols] = value

    stage(net.relay, 0)
    stage(net.spread_plane, 1)
    stage(net.spread_z, 1)
    stage(net.take_slabs, 0)
    stage(net.take_far, 0, 0)
    stage(net.take_far, 0, 1)
    stage(net.take_far, 0, 2)
    net.finish_near(0)
    loads[5].wait()
    product(0, (0, 1))
    net.finish_rest(0)
    product(0, (7, 2))
    product(0, (6, 3))
    product(0, (5, 4))
    stage(net.take_slabs, 1)
    stage(net.take_far, 1, 0)
    net.finish_near(1)
    product(1, (0, 1))
    stage(net.take_far, 1, 1)
    product(1, (7,))
    stage(net.take_far, 1, 2)
    net.finish_rest(1)
    all_seven(parts, 0).wait_send()
    all_seven(whole, 2).wait_send()
    net.leave(0)
    net.leave(1)


def write_kernel(first, second, acc, lhs, gathered, out1, out2, out, stage, sems):
    z = lax.div(lax.axis_index("wide"), NY)
    copies = [
        pltpu.make_async_copy(first, out1, sems.at[8]),
        pltpu.make_async_copy(second, out2, sems.at[9]),
    ]
    for copy in copies:
        copy.start()
    for steps in NEAR_STEPS:
        for dz, cols in zip(steps, columns_of(z, steps)):
            copies.append(
                pltpu.make_async_copy(acc.at[:, :, cols], out.at[:, :, cols], sems.at[dz])
            )
            copies[-1].start()
    for steps in REST_STEPS:
        columns = columns_of(z, steps)
        for plane in range(2):
            for cols, value in zip(columns, update(acc, lhs, gathered, 1, plane, steps, columns)):
                stage[plane, :, cols] = value
        for dz, cols in zip(steps, columns):
            copies.append(
                pltpu.make_async_copy(stage.at[:, :, cols], out.at[:, :, cols], sems.at[dz])
            )
            copies[-1].start()
    for copy in copies:
        copy.wait()


def body(inverse_first, inverse_second, coupling, head_rhs, panel_rows, trail_rhs):
    dma = pltpu.SemaphoreType.DMA
    held = pl.pallas_call(
        gather_kernel,
        out_shape=(
            pltpu.VMEM((2, 32, 64), F32),
            pltpu.VMEM((2, 32, 64), F32),
            pltpu.VMEM((2, 512, 1024), F32),
            pltpu.VMEM((2, 2, 512, 1024), BF16),
            pltpu.VMEM((2, 2, NZ, NY, NX, 32, 128), BF16),
        ),
        in_specs=[pl.BlockSpec(memory_space=pltpu.HBM)] * 6,
        out_specs=[pl.BlockSpec(memory_space=pltpu.VMEM)] * 5,
        scratch_shapes=[
            pltpu.VMEM((128, 512), F32),
            pltpu.VMEM((128, 512), F32),
            pltpu.VMEM((128, 512), F32),
            pltpu.VMEM((64, 1024), F32),
            pltpu.VMEM((512, 2048), BF16),
            pltpu.VMEM((8, 8, 512), F32),
            pltpu.VMEM((8, 8, 512), F32),
            pltpu.VMEM((8, 8, 512), F32),
            pltpu.VMEM((2, 128, 512), BF16),
            dma((6,)),
            dma((4,)),
            dma((2, 3)),
            dma((2, 9)),
        ],
        compiler_params=pltpu.CompilerParams(
            collective_id=0, has_side_effects=True, vmem_limit_bytes=24 << 20
        ),
        cost_estimate=pl.CostEstimate(flops=2 << 30, bytes_accessed=8 << 20, transcendentals=0),
    )(
        *(
            pltpu.with_memory_space_constraint(operand, pltpu.HBM)
            for operand in (
                inverse_first.reshape(128, 512),
                inverse_second.reshape(128, 512),
                jnp.transpose(coupling, (0, 2, 1)).reshape(128, 512),
                jnp.transpose(head_rhs, (0, 2, 1)).reshape(64, 1024),
                panel_rows,
                trail_rhs,
            )
        )
    )
    first, second, updated = pl.pallas_call(
        write_kernel,
        out_shape=(
            jax.ShapeDtypeStruct((2, 32, 64), F32),
            jax.ShapeDtypeStruct((2, 32, 64), F32),
            jax.ShapeDtypeStruct((2, 512, 1024), F32),
        ),
        in_specs=[pl.BlockSpec(memory_space=pltpu.VMEM)] * 5,
        out_specs=[pl.BlockSpec(memory_space=pltpu.HBM)] * 3,
        scratch_shapes=[pltpu.VMEM((2, 512, 1024), F32), dma((10,))],
        compiler_params=pltpu.CompilerParams(vmem_limit_bytes=16 << 20),
        cost_estimate=pl.CostEstimate(flops=2 << 30, bytes_accessed=4 << 20, transcendentals=0),
    )(*(pltpu.with_memory_space_constraint(value, pltpu.VMEM) for value in held))
    return jnp.transpose(first, (0, 2, 1)), jnp.transpose(second, (0, 2, 1)), updated


def solution(mesh):
    return jax.shard_map(
        body,
        mesh=mesh,
        in_specs=(
            P(None, "rows", None),
            P(None, "rows", None),
            P(None, None, "rows"),
            P(None, None, "wide"),
            P(("rows", "wide"), None),
            P(None, ("rows", "wide"), None),
        ),
        out_specs=(
            P(None, "rows", "wide"),
            P(None, "rows", "wide"),
            P(None, ("rows", "wide"), None),
        ),
        check_vma=False,
    )
```

```python
import functools

import jax
import jax.numpy as jnp
from jax import lax
from jax.experimental import pallas as pl
from jax.experimental.pallas import tpu as pltpu
from jax.sharding import PartitionSpec as P

MESH = pl.DeviceIdType.MESH
F32 = jnp.float32
BF16 = jnp.bfloat16
NX, NY, NZ = 4, 4, 8
NEAR = ((2, 2), (2, 1))
RELAY = (0,)
PLANE = sorted(
    ((i, j) for i in range(NX) for j in range(NY) if i or j),
    key=lambda p: -(min(p[0], NX - p[0]) + min(p[1], NY - p[1])),
)
SENT_FIRST, SENT, SENT_ON = range(3)
OVER_PLANE, ALONG_Z, SLABS, NEAR_ON, SLABS_ON, FAR, FAR_ON = 0, 1, 1, 4, 5, 6, 10
NT = (((1,), (1,)), ((), ()))
NN = (((1,), (0,)), ((), ()))


def split(value):
    high = value.astype(BF16)
    return high, (value - high.astype(F32)).astype(BF16)


def dot3(left, right, dims):
    (left_high, left_low), (right_high, right_low) = left, right
    dot = functools.partial(lax.dot_general, dimension_numbers=dims, preferred_element_type=F32)
    return dot(left_high, right_high) + (dot(left_low, right_high) + dot(left_high, right_low))


def swap(value):
    return pltpu.roll(value, 64, 1)


def first_lanes(shape):
    return lax.broadcasted_iota(jnp.int32, shape, 1) < 64


def solve(rhs, inverse):
    both = dot3(split(rhs), inverse, NT)
    top, low = both[:32], swap(both[32:])
    return jnp.where(first_lanes(top.shape), top - low, top + low)


class Net:
    def __init__(self, gathered, sems):
        self.g, self.sems = gathered, sems
        self.rows, self.wide = lax.axis_index("rows"), lax.axis_index("wide")
        self.x, self.core = lax.div(self.rows, 2), lax.rem(self.rows, 2)
        self.z, self.y = lax.div(self.wide, NY), lax.rem(self.wide, NY)

    def on_rows(self, j):
        return lax.rem(self.rows + j, 2 * NX), self.wide

    def on_plane(self, i, j):
        x, y = lax.rem(self.x + i, NX), lax.rem(self.y + j, NY)
        return 2 * x + self.core, self.z * NY + y

    def on_z(self, j):
        return self.rows, lax.rem(self.z + j, NZ) * NY + self.y

    def sibling(self):
        return self.rows + 1 - 2 * self.core, self.wide

    def copy(self, src, dst, half, sent, landed, to):
        send, recv = self.sems
        return pltpu.make_async_remote_copy(
            src_ref=src,
            dst_ref=dst,
            send_sem=send.at[half, sent],
            recv_sem=recv.at[half, landed],
            device_id=to,
            device_id_type=MESH,
        )

    def block(self, half, dz, i=0, j=0, core=None):
        x, y = lax.rem(self.x + (NX - i), NX), lax.rem(self.y + (NY - j), NY)
        return self.g.at[half, self.core if core is None else core, dz, y, x]

    def slab(self, half, dz):
        return self.g.at[half, self.core, dz]

    def far(self, half, near):
        return self.block(half, pl.ds(near + 1, NZ - 1 - 2 * near))

    def along_z(self, half, j):
        src, dst = self.block(half, 0), self.block(half, NZ - j)
        return self.copy(src, dst, half, SENT, ALONG_Z, self.on_z(j))

    def over_plane(self, half, i, j):
        ref = self.block(half, 0)
        return self.copy(ref, ref, half, SENT_FIRST, OVER_PLANE, self.on_plane(i, j))

    def slabs_along_z(self, half, step):
        for j in (step, NZ - step):
            src, dst = self.slab(half, 0), self.slab(half, NZ - j)
            yield self.copy(src, dst, half, SENT, SLABS + step, self.on_z(j))

    def far_over(self, half, near, i, j):
        ref = self.far(half, near)
        return self.copy(ref, ref, half, SENT, FAR + i, self.on_plane(i, j))

    def hand_on(self, half, ref, landed):
        self.copy(ref, ref, half, SENT_ON, landed, self.sibling()).start()

    def wait(self, half, blocks, sent=None, landed=None):
        z, y, x = blocks
        ref = self.g.at[half, self.core, pl.ds(0, z), pl.ds(0, y), pl.ds(0, x)]
        copy = self.copy(ref, ref, half, sent or 0, landed or 0, self.sibling())
        if landed is None:
            copy.wait_send()
        else:
            copy.wait_recv()


    def open(self, half, near):
        for j in far_steps(near):
            self.along_z(half, j).start()
        for i, j in PLANE:
            self.over_plane(half, i, j).start()

    def spread_plane(self, half, near):
        self.wait(half, (5, 3, 1), landed=OVER_PLANE)
        for step in range(1, (1 if half in RELAY else near) + 1):
            for copy in self.slabs_along_z(half, step):
                copy.start()
        self.hand_on(half, self.slab(half, 0), NEAR_ON)

    def relay(self, half, near):
        self.wait(half, (2, NY, NX), landed=SLABS + 1)
        for dz, way in ((NZ - 1, 1), (1, NZ - 1)):
            src, dst = self.slab(half, dz), self.slab(half, 2 * dz % NZ)
            self.copy(src, dst, half, SENT, SLABS + 2, self.on_z(way)).start()
        for dz in (1, NZ - 1):
            self.hand_on(half, self.slab(half, dz), NEAR_ON)

    def spread_z(self, half, near):
        self.wait(half, (NZ - 1 - 2 * near, 1, 1), landed=ALONG_Z)
        for i, j in [(2, 2), (1, 2), (3, 2), (0, 2), (2, 1), (1, 1), (3, 1), (0, 1), (2, 3), (1, 3), (3, 3), (0, 3), (2, 0), (1, 0), (3, 0)]:
            self.far_over(half, near, i, j).start()

    def take_slabs(self, half, near):
        for step in range(2 if half in RELAY else 1, near + 1):
            self.wait(half, (2, NY, NX), landed=SLABS + step)
            for dz in (step, NZ - step):
                self.hand_on(half, self.slab(half, dz), NEAR_ON if step == 1 else SLABS_ON)

    def take_far(self, half, near, i):
        count = NZ - 1 - 2 * near
        self.wait(half, (count, NY - 1 if i == 0 else NY, 1), landed=FAR + i)
        ref = self.g.at[half, self.core, pl.ds(near + 1, count), :, lax.rem(self.x + (NX - i), NX)]
        self.hand_on(half, ref, FAR_ON + i)

    def finish_near(self, half):
        self.wait(half, (3, NY, NX), landed=NEAR_ON)

    def finish_slabs(self, half, near):
        if near > 1:
            self.wait(half, (2 * near - 2, NY, NX), landed=SLABS_ON)

    def finish_far(self, half, near, i):
        self.wait(half, (NZ - 1 - 2 * near, NY, 1), landed=FAR_ON + i)

    def leave(self, half):
        self.wait(half, (5, 3, 1), sent=SENT_FIRST)
        self.wait(half, (NZ - 1, NY, NX), sent=SENT)
        self.wait(half, (NZ, NY, NX), sent=SENT_ON)


def far_steps(near):
    return sorted(range(near + 1, NZ - near), key=lambda j: -min(j, NZ - j))


def update(acc, out, lhs, gathered, half, steps, columns, core=None, planes=(0, 1)):
    right = jnp.concatenate(
        [
            jnp.concatenate([gathered[half, c, dz, :, x].reshape(128, 128) for dz in steps], 0)
            for c in (range(2) if core is None else [core])
            for x in range(NX)
        ],
        1,
    )
    for plane in planes:
        if core is None:
            left = lhs[half, plane]
        else:
            left = lhs[half, plane, :, pl.ds(pl.multiple_of(128 * NX * core, 128 * NX), 128 * NX)]
        product = lax.dot_general(left, right, NT, preferred_element_type=F32)
        for at, cols in enumerate(columns):
            out[plane, :, cols] = acc[plane, :, cols] + product[:, 128 * at : 128 * (at + 1)]


def columns_of(z, steps):
    return [pl.ds(pl.multiple_of(128 * lax.rem(z + dz, NZ), 128), 128) for dz in steps]


NEAR_STEPS, REST_STEPS = ((0, 1), (7,)), ((2, 3), (4, 5), (6,))


def gather_kernel(
    inv1_hbm, inv2_hbm, coup_hbm, head_hbm, panel_hbm, trail_hbm,
    out1, out2, acc, lhs, gathered,
    inv1, inv2, coup, head, panel, parts, sums, whole, inv2_split,
    local, sum_sems, send_sems, recv_sems,
):
    loads = [
        pltpu.make_async_copy(src, dst, local.at[i])
        for i, (src, dst) in enumerate(
            [
                (head_hbm, head),
                (inv1_hbm, inv1),
                (coup_hbm, coup),
                (inv2_hbm, inv2),
                (panel_hbm, panel),
                (trail_hbm, acc),
            ]
        )
    ]
    for load in loads[:3]:
        load.start()

    net = Net(gathered, (send_sems, recv_sems))
    rows, x, core = net.rows, net.x, net.core

    def stage(step, half, *more, other=False):
        near = NEAR[half][::-1] if other else NEAR[half]
        if near[0] == near[1]:
            step(half, near[0], *more)
        else:
            for at in range(2):
                pl.when(core == at)(functools.partial(step, half, near[at], *more))

    barrier = pltpu.get_barrier_semaphore()
    peers = [net.on_z(j) for j in far_steps(0)]
    peers += [net.on_plane(i, j) for i, j in PLANE if j]
    peers += [net.on_rows(j) for j in range(1, 2 * NX)]
    for peer in peers:
        pl.semaphore_signal(barrier, inc=1, device_id=peer, device_id_type=MESH)

    loads[0].wait()
    loads[1].wait()
    for load in loads[3:]:
        load.start()
    solved = solve(head[:, :512], split(inv1[...]))
    gathered[0, core, 0, net.y, x] = solved.astype(BF16)
    first = first_lanes(solved.shape)
    turned = swap(solved)
    out1[0] = solved[:, :64]
    out1[1] = turned[:, :64]
    loads[2].wait()
    left = jnp.concatenate([jnp.where(first, solved, -solved), turned], 0)
    parts[...] = dot3(split(left), split(coup[...]), NN).reshape(parts.shape)

    pl.semaphore_wait(barrier, len(peers))

    def reduce_copy(j):
        to = net.on_rows(j)
        return pltpu.make_async_remote_copy(
            src_ref=parts.at[to[0]],
            dst_ref=sums.at[j],
            send_sem=sum_sems.at[0],
            recv_sem=sum_sems.at[1],
            device_id=to,
            device_id_type=MESH,
        )

    def share_copy(j):
        ref = whole.at[rows]
        return pltpu.make_async_remote_copy(
            src_ref=ref,
            dst_ref=ref,
            send_sem=sum_sems.at[2],
            recv_sem=sum_sems.at[3],
            device_id=net.on_rows(j),
            device_id_type=MESH,
        )

    def all_seven(ref, at):
        ref = ref.at[pl.ds(1, 2 * NX - 1)]
        return pltpu.make_async_remote_copy(
            src_ref=ref,
            dst_ref=ref,
            send_sem=sum_sems.at[at],
            recv_sem=sum_sems.at[at + 1],
            device_id=net.sibling(),
            device_id_type=MESH,
        )

    order = (4, 3, 5, 2, 6, 1, 7)
    for j in order:
        reduce_copy(j).start()
    stage(net.open, 0)

    loads[4].wait()
    for half in range(2):
        for at in range(NX):
            base = 512 * half + 128 * at
            real = panel[:, base : base + 128].astype(F32)
            imag = panel[:, 1024 + base : 1024 + base + 128].astype(F32)
            head_lanes = first_lanes(real.shape)
            real_turned, imag_turned = swap(real), swap(imag)
            for c in range(2):
                k = (NX * c + at) * 128
                if c == 0:
                    plane0 = jnp.where(head_lanes, -real, imag_turned)
                    plane1 = jnp.where(head_lanes, -imag, -real_turned)
                else:
                    plane0 = jnp.where(head_lanes, -real_turned, imag)
                    plane1 = jnp.where(head_lanes, -imag_turned, -real)
                lhs[half, 0, :, k : k + 128] = plane0.astype(BF16)
                lhs[half, 1, :, k : k + 128] = plane1.astype(BF16)

    loads[3].wait()
    inv2_split[0], inv2_split[1] = split(inv2[...])

    all_seven(sums, 0).wait_recv()
    total = parts[rows]
    for j in range(1, 2 * NX):
        total += sums[j]
    whole[rows] = head[pl.ds(pl.multiple_of(8 * rows, 8), 8), 512:] - total
    for j in order:
        share_copy(j).start()

    stage(net.spread_plane, 0)
    stage(net.spread_z, 0)
    all_seven(whole, 2).wait_recv()
    solved = solve(whole[...].reshape(64, 512), (inv2_split[0], inv2_split[1]))
    gathered[1, core, 0, net.y, x] = solved.astype(BF16)
    stage(net.open, 1)
    out2[0] = solved[:, :64]
    out2[1] = swap(solved)[:, :64]

    def product(half, steps, *one):
        update(acc, acc, lhs, gathered, half, steps, columns_of(net.z, steps), *one)

    stage(net.relay, 0)
    stage(net.spread_plane, 1)
    stage(net.spread_z, 1)
    stage(net.take_slabs, 0)
    stage(net.take_far, 0, 0)
    stage(net.take_far, 0, 1)
    stage(net.take_far, 0, 3)
    stage(net.take_far, 0, 2)
    net.finish_near(0)
    loads[5].wait()
    product(0, (0, 1))
    stage(net.finish_slabs, 0, other=True)
    stage(net.finish_far, 0, 0, other=True)
    stage(net.finish_far, 0, 1, other=True)
    stage(net.finish_far, 0, 3, other=True)
    stage(net.finish_far, 0, 2, other=True)
    product(0, (7, 2))
    product(0, (6, 3))
    product(0, (5, 4))
    stage(net.take_slabs, 1)
    stage(net.take_far, 1, 0)
    stage(net.take_far, 1, 1)
    stage(net.take_far, 1, 3)
    stage(net.take_far, 1, 2)
    net.finish_near(1)
    product(1, (0, 1))
    product(1, (7,))
    for steps in REST_STEPS:
        product(1, steps, core)
    stage(net.finish_slabs, 1, other=True)
    stage(net.finish_far, 1, 0, other=True)
    stage(net.finish_far, 1, 1, other=True)
    stage(net.finish_far, 1, 3, other=True)
    stage(net.finish_far, 1, 2, other=True)
    all_seven(parts, 0).wait_send()
    all_seven(whole, 2).wait_send()
    net.leave(0)
    net.leave(1)


def write_kernel(first, second, acc, lhs, gathered, out1, out2, out, stage, sems):
    core, z = lax.rem(lax.axis_index("rows"), 2), lax.div(lax.axis_index("wide"), NY)
    copies = [
        pltpu.make_async_copy(first, out1, sems.at[8]),
        pltpu.make_async_copy(second, out2, sems.at[9]),
    ]
    for copy in copies:
        copy.start()
    for steps in NEAR_STEPS:
        for dz, cols in zip(steps, columns_of(z, steps)):
            copies.append(
                pltpu.make_async_copy(acc.at[:, :, cols], out.at[:, :, cols], sems.at[dz])
            )
            copies[-1].start()
    for steps in REST_STEPS:
        columns = columns_of(z, steps)
        for plane in range(2):
            update(acc, stage, lhs, gathered, 1, steps, columns, 1 - core, (plane,))
            for dz, cols in zip(steps, columns):
                copies.append(
                    pltpu.make_async_copy(stage.at[plane, :, cols], out.at[plane, :, cols], sems.at[10 + 8 * plane + dz])
                )
                copies[-1].start(priority=plane)
    for copy in copies:
        copy.wait()


def body(inverse_first, inverse_second, coupling, head_rhs, panel_rows, trail_rhs):
    dma = pltpu.SemaphoreType.DMA
    held = pl.pallas_call(
        gather_kernel,
        out_shape=(
            pltpu.VMEM((2, 32, 64), F32),
            pltpu.VMEM((2, 32, 64), F32),
            pltpu.VMEM((2, 512, 1024), F32),
            pltpu.VMEM((2, 2, 512, 1024), BF16),
            pltpu.VMEM((2, 2, NZ, NY, NX, 32, 128), BF16),
        ),
        in_specs=[pl.BlockSpec(memory_space=pltpu.HBM)] * 6,
        out_specs=[pl.BlockSpec(memory_space=pltpu.VMEM)] * 5,
        scratch_shapes=[
            pltpu.VMEM((128, 512), F32),
            pltpu.VMEM((128, 512), F32),
            pltpu.VMEM((128, 512), F32),
            pltpu.VMEM((64, 1024), F32),
            pltpu.VMEM((512, 2048), BF16),
            pltpu.VMEM((8, 8, 512), F32),
            pltpu.VMEM((8, 8, 512), F32),
            pltpu.VMEM((8, 8, 512), F32),
            pltpu.VMEM((2, 128, 512), BF16),
            dma((6,)),
            dma((4,)),
            dma((2, 3)),
            dma((2, 14)),
        ],
        compiler_params=pltpu.CompilerParams(
            collective_id=0, has_side_effects=True, vmem_limit_bytes=24 << 20
        ),
        cost_estimate=pl.CostEstimate(flops=2 << 30, bytes_accessed=8 << 20, transcendentals=0),
    )(
        *(
            pltpu.with_memory_space_constraint(operand, pltpu.HBM)
            for operand in (
                inverse_first.reshape(128, 512),
                inverse_second.reshape(128, 512),
                jnp.transpose(coupling, (0, 2, 1)).reshape(128, 512),
                jnp.transpose(head_rhs, (0, 2, 1)).reshape(64, 1024),
                panel_rows,
                trail_rhs,
            )
        )
    )
    first, second, updated = pl.pallas_call(
        write_kernel,
        out_shape=(
            jax.ShapeDtypeStruct((2, 32, 64), F32),
            jax.ShapeDtypeStruct((2, 32, 64), F32),
            jax.ShapeDtypeStruct((2, 512, 1024), F32),
        ),
        in_specs=[pl.BlockSpec(memory_space=pltpu.VMEM)] * 5,
        out_specs=[pl.BlockSpec(memory_space=pltpu.HBM)] * 3,
        scratch_shapes=[pltpu.VMEM((2, 512, 1024), F32), dma((26,))],
        compiler_params=pltpu.CompilerParams(vmem_limit_bytes=16 << 20),
        cost_estimate=pl.CostEstimate(flops=2 << 30, bytes_accessed=4 << 20, transcendentals=0),
    )(*(pltpu.with_memory_space_constraint(value, pltpu.VMEM) for value in held))
    return jnp.transpose(first, (0, 2, 1)), jnp.transpose(second, (0, 2, 1)), updated


def solution(mesh):
    return jax.shard_map(
        body,
        mesh=mesh,
        in_specs=(
            P(None, "rows", None),
            P(None, "rows", None),
            P(None, None, "rows"),
            P(None, None, "wide"),
            P(("rows", "wide"), None),
            P(None, ("rows", "wide"), None),
        ),
        out_specs=(
            P(None, "rows", "wide"),
            P(None, "rows", "wide"),
            P(None, ("rows", "wide"), None),
        ),
        check_vma=False,
    )
```

```python
import functools

import jax
import jax.numpy as jnp
from jax import lax
from jax.experimental import pallas as pl
from jax.experimental.pallas import tpu as pltpu
from jax.sharding import PartitionSpec as P

MESH = pl.DeviceIdType.MESH
F32 = jnp.float32
BF16 = jnp.bfloat16
NX, NY, NZ = 4, 4, 8
NEAR = ((2, 2), (2, 1))
RELAY = (0,)
PLANE = sorted(
    ((i, j) for i in range(NX) for j in range(NY) if i or j),
    key=lambda p: -(min(p[0], NX - p[0]) + min(p[1], NY - p[1])),
)
SENT_FIRST, SENT, SENT_ON = range(3)
OVER_PLANE, ALONG_Z, SLABS, NEAR_ON, SLABS_ON, FAR, FAR_ON = 0, 1, 1, 4, 5, 6, 10
NT = (((1,), (1,)), ((), ()))
NN = (((1,), (0,)), ((), ()))


def split(value):
    high = value.astype(BF16)
    return high, (value - high.astype(F32)).astype(BF16)


def dot3(left, right, dims):
    (left_high, left_low), (right_high, right_low) = left, right
    dot = functools.partial(lax.dot_general, dimension_numbers=dims, preferred_element_type=F32)
    return dot(left_high, right_high) + (dot(left_low, right_high) + dot(left_high, right_low))


def swap(value):
    return pltpu.roll(value, 64, 1)


def first_lanes(shape):
    return lax.broadcasted_iota(jnp.int32, shape, 1) < 64


def solve(rhs, inverse):
    both = dot3(split(rhs), inverse, NT)
    top, low = both[:32], swap(both[32:])
    return jnp.where(first_lanes(top.shape), top - low, top + low)


class Net:
    def __init__(self, gathered, sems):
        self.g, self.sems = gathered, sems
        self.rows, self.wide = lax.axis_index("rows"), lax.axis_index("wide")
        self.x, self.core = lax.div(self.rows, 2), lax.rem(self.rows, 2)
        self.z, self.y = lax.div(self.wide, NY), lax.rem(self.wide, NY)

    def on_rows(self, j):
        return lax.rem(self.rows + j, 2 * NX), self.wide

    def on_plane(self, i, j):
        x, y = lax.rem(self.x + i, NX), lax.rem(self.y + j, NY)
        return 2 * x + self.core, self.z * NY + y

    def on_z(self, j):
        return self.rows, lax.rem(self.z + j, NZ) * NY + self.y

    def sibling(self):
        return self.rows + 1 - 2 * self.core, self.wide

    def copy(self, src, dst, half, sent, landed, to):
        send, recv = self.sems
        return pltpu.make_async_remote_copy(
            src_ref=src,
            dst_ref=dst,
            send_sem=send.at[half, sent],
            recv_sem=recv.at[half, landed],
            device_id=to,
            device_id_type=MESH,
        )

    def block(self, half, dz, i=0, j=0, core=None):
        x, y = lax.rem(self.x + (NX - i), NX), lax.rem(self.y + (NY - j), NY)
        return self.g.at[half, self.core if core is None else core, dz, y, x]

    def slab(self, half, dz):
        return self.g.at[half, self.core, dz]

    def far(self, half, near):
        return self.block(half, pl.ds(near + 1, NZ - 1 - 2 * near))

    def along_z(self, half, j):
        src, dst = self.block(half, 0), self.block(half, NZ - j)
        return self.copy(src, dst, half, SENT, ALONG_Z, self.on_z(j))

    def over_plane(self, half, i, j):
        ref = self.block(half, 0)
        return self.copy(ref, ref, half, SENT_FIRST, OVER_PLANE, self.on_plane(i, j))

    def slabs_along_z(self, half, step):
        for j in (step, NZ - step):
            src, dst = self.slab(half, 0), self.slab(half, NZ - j)
            yield self.copy(src, dst, half, SENT, SLABS + step, self.on_z(j))

    def far_over(self, half, near, i, j):
        ref = self.far(half, near)
        return self.copy(ref, ref, half, SENT, FAR + i, self.on_plane(i, j))

    def hand_on(self, half, ref, landed):
        self.copy(ref, ref, half, SENT_ON, landed, self.sibling()).start()

    def wait(self, half, blocks, sent=None, landed=None):
        z, y, x = blocks
        ref = self.g.at[half, self.core, pl.ds(0, z), pl.ds(0, y), pl.ds(0, x)]
        copy = self.copy(ref, ref, half, sent or 0, landed or 0, self.sibling())
        if landed is None:
            copy.wait_send()
        else:
            copy.wait_recv()


    def open(self, half, near):
        for j in far_steps(near):
            self.along_z(half, j).start()
        for i, j in PLANE:
            self.over_plane(half, i, j).start()

    def spread_plane(self, half, near):
        self.wait(half, (5, 3, 1), landed=OVER_PLANE)
        for step in range(1, (1 if half in RELAY else near) + 1):
            for copy in self.slabs_along_z(half, step):
                copy.start()
        self.hand_on(half, self.slab(half, 0), NEAR_ON)

    def relay(self, half, near):
        self.wait(half, (2, NY, NX), landed=SLABS + 1)
        for dz, way in ((NZ - 1, 1), (1, NZ - 1)):
            src, dst = self.slab(half, dz), self.slab(half, 2 * dz % NZ)
            self.copy(src, dst, half, SENT, SLABS + 2, self.on_z(way)).start()
        for dz in (1, NZ - 1):
            self.hand_on(half, self.slab(half, dz), NEAR_ON)

    def spread_z(self, half, near):
        self.wait(half, (NZ - 1 - 2 * near, 1, 1), landed=ALONG_Z)
        for i, j in [(2, 2), (1, 2), (3, 2), (0, 2), (2, 1), (1, 1), (3, 1), (0, 1), (2, 3), (1, 3), (3, 3), (0, 3), (2, 0), (1, 0), (3, 0)]:
            self.far_over(half, near, i, j).start()

    def take_slabs(self, half, near):
        for step in range(2 if half in RELAY else 1, near + 1):
            self.wait(half, (2, NY, NX), landed=SLABS + step)
            for dz in (step, NZ - step):
                self.hand_on(half, self.slab(half, dz), NEAR_ON if step == 1 else SLABS_ON)

    def take_far(self, half, near, i):
        count = NZ - 1 - 2 * near
        self.wait(half, (count, NY - 1 if i == 0 else NY, 1), landed=FAR + i)
        ref = self.g.at[half, self.core, pl.ds(near + 1, count), :, lax.rem(self.x + (NX - i), NX)]
        self.hand_on(half, ref, FAR_ON + i)

    def finish_near(self, half):
        self.wait(half, (3, NY, NX), landed=NEAR_ON)

    def finish_slabs(self, half, near):
        if near > 1:
            self.wait(half, (2 * near - 2, NY, NX), landed=SLABS_ON)

    def finish_far(self, half, near, i):
        self.wait(half, (NZ - 1 - 2 * near, NY, 1), landed=FAR_ON + i)

    def leave(self, half):
        self.wait(half, (5, 3, 1), sent=SENT_FIRST)
        self.wait(half, (NZ - 1, NY, NX), sent=SENT)
        self.wait(half, (NZ, NY, NX), sent=SENT_ON)


def far_steps(near):
    return sorted(range(near + 1, NZ - near), key=lambda j: -min(j, NZ - j))


def update(acc, out, lhs, gathered, half, steps, columns, core=None, planes=(0, 1)):
    right = jnp.concatenate(
        [
            jnp.concatenate([gathered[half, c, dz, :, x].reshape(128, 128) for dz in steps], 0)
            for c in (range(2) if core is None else [core])
            for x in range(NX)
        ],
        1,
    )
    for plane in planes:
        if core is None:
            left = lhs[half, plane]
        else:
            left = lhs[half, plane, :, pl.ds(pl.multiple_of(128 * NX * core, 128 * NX), 128 * NX)]
        product = lax.dot_general(left, right, NT, preferred_element_type=F32)
        for at, cols in enumerate(columns):
            out[plane, :, cols] = acc[plane, :, cols] + product[:, 128 * at : 128 * (at + 1)]


def columns_of(z, steps):
    return [pl.ds(pl.multiple_of(128 * lax.rem(z + dz, NZ), 128), 128) for dz in steps]


NEAR_STEPS, REST_STEPS = ((0, 1), (7,)), ((2, 3), (4, 5), (6,))


def gather_kernel(
    inv1_hbm, inv2_hbm, coup_hbm, head_hbm, panel_hbm, trail_hbm,
    out1, out2, acc, lhs, gathered,
    inv1, inv2, coup, head, panel, parts, sums, whole, inv2_split,
    local, sum_sems, send_sems, recv_sems,
):
    loads = [
        pltpu.make_async_copy(src, dst, local.at[i])
        for i, (src, dst) in enumerate(
            [
                (head_hbm, head),
                (inv1_hbm, inv1),
                (coup_hbm, coup),
                (inv2_hbm, inv2),
                (panel_hbm, panel),
                (trail_hbm, acc),
            ]
        )
    ]
    for load in loads[:3]:
        load.start()

    net = Net(gathered, (send_sems, recv_sems))
    rows, x, core = net.rows, net.x, net.core

    def stage(step, half, *more, other=False):
        near = NEAR[half][::-1] if other else NEAR[half]
        if near[0] == near[1]:
            step(half, near[0], *more)
        else:
            for at in range(2):
                pl.when(core == at)(functools.partial(step, half, near[at], *more))

    barrier = pltpu.get_barrier_semaphore()
    peers = [net.on_z(j) for j in far_steps(0)]
    peers += [net.on_plane(i, j) for i, j in PLANE if j]
    peers += [net.on_rows(j) for j in range(1, 2 * NX)]
    for peer in peers:
        pl.semaphore_signal(barrier, inc=1, device_id=peer, device_id_type=MESH)

    loads[0].wait()
    loads[1].wait()
    for load in loads[3:]:
        load.start()
    solved = solve(head[:, :512], split(inv1[...]))
    gathered[0, core, 0, net.y, x] = solved.astype(BF16)
    first = first_lanes(solved.shape)
    turned = swap(solved)
    out1[0] = solved[:, :64]
    out1[1] = turned[:, :64]
    loads[2].wait()
    left = jnp.concatenate([jnp.where(first, solved, -solved), turned], 0)
    parts[...] = dot3(split(left), split(coup[...]), NN).reshape(parts.shape)

    pl.semaphore_wait(barrier, len(peers))

    def reduce_copy(j):
        to = net.on_rows(j)
        return pltpu.make_async_remote_copy(
            src_ref=parts.at[to[0]],
            dst_ref=sums.at[j],
            send_sem=sum_sems.at[0],
            recv_sem=sum_sems.at[1],
            device_id=to,
            device_id_type=MESH,
        )

    def share_copy(j):
        ref = whole.at[rows]
        return pltpu.make_async_remote_copy(
            src_ref=ref,
            dst_ref=ref,
            send_sem=sum_sems.at[2],
            recv_sem=sum_sems.at[3],
            device_id=net.on_rows(j),
            device_id_type=MESH,
        )

    def all_seven(ref, at):
        ref = ref.at[pl.ds(1, 2 * NX - 1)]
        return pltpu.make_async_remote_copy(
            src_ref=ref,
            dst_ref=ref,
            send_sem=sum_sems.at[at],
            recv_sem=sum_sems.at[at + 1],
            device_id=net.sibling(),
            device_id_type=MESH,
        )

    order = (4, 3, 5, 2, 6, 1, 7)
    for j in order:
        reduce_copy(j).start()
    stage(net.open, 0)

    loads[4].wait()
    loads[3].wait()
    inv2_split[0], inv2_split[1] = split(inv2[...])

    all_seven(sums, 0).wait_recv()
    total = parts[rows]
    for j in range(1, 2 * NX):
        total += sums[j]
    whole[rows] = head[pl.ds(pl.multiple_of(8 * rows, 8), 8), 512:] - total
    for j in order:
        share_copy(j).start()

    stage(net.spread_plane, 0)
    stage(net.spread_z, 0)
    for half in range(2):
        for at in range(NX):
            base = 512 * half + 128 * at
            real = panel[:, base : base + 128].astype(F32)
            imag = panel[:, 1024 + base : 1024 + base + 128].astype(F32)
            head_lanes = first_lanes(real.shape)
            real_turned, imag_turned = swap(real), swap(imag)
            for c in range(2):
                k = (NX * c + at) * 128
                if c == 0:
                    plane0 = jnp.where(head_lanes, -real, imag_turned)
                    plane1 = jnp.where(head_lanes, -imag, -real_turned)
                else:
                    plane0 = jnp.where(head_lanes, -real_turned, imag)
                    plane1 = jnp.where(head_lanes, -imag_turned, -real)
                lhs[half, 0, :, k : k + 128] = plane0.astype(BF16)
                lhs[half, 1, :, k : k + 128] = plane1.astype(BF16)

    all_seven(whole, 2).wait_recv()
    solved = solve(whole[...].reshape(64, 512), (inv2_split[0], inv2_split[1]))
    gathered[1, core, 0, net.y, x] = solved.astype(BF16)
    stage(net.open, 1)
    out2[0] = solved[:, :64]
    out2[1] = swap(solved)[:, :64]

    def product(half, steps, *one):
        update(acc, acc, lhs, gathered, half, steps, columns_of(net.z, steps), *one)

    stage(net.relay, 0)
    stage(net.spread_z, 1)
    stage(net.spread_plane, 1)
    stage(net.take_slabs, 0)
    stage(net.take_far, 0, 0)
    stage(net.take_far, 0, 1)
    stage(net.take_far, 0, 3)
    stage(net.take_far, 0, 2)
    net.finish_near(0)
    loads[5].wait()
    product(0, (0, 1))
    stage(net.finish_slabs, 0, other=True)
    stage(net.finish_far, 0, 0, other=True)
    stage(net.finish_far, 0, 1, other=True)
    stage(net.finish_far, 0, 3, other=True)
    stage(net.finish_far, 0, 2, other=True)
    product(0, (7, 2))
    product(0, (6, 3))
    product(0, (5, 4))
    stage(net.take_slabs, 1)
    stage(net.take_far, 1, 0)
    stage(net.take_far, 1, 1)
    stage(net.take_far, 1, 3)
    stage(net.take_far, 1, 2)
    net.finish_near(1)
    product(1, (0, 1))
    product(1, (7,))
    for steps in REST_STEPS:
        product(1, steps, core)
    stage(net.finish_slabs, 1, other=True)
    stage(net.finish_far, 1, 0, other=True)
    stage(net.finish_far, 1, 1, other=True)
    stage(net.finish_far, 1, 3, other=True)
    stage(net.finish_far, 1, 2, other=True)
    all_seven(parts, 0).wait_send()
    all_seven(whole, 2).wait_send()
    net.leave(0)
    net.leave(1)


def write_kernel(first, second, acc, lhs, gathered, out1, out2, out, stage, sems):
    core, z = lax.rem(lax.axis_index("rows"), 2), lax.div(lax.axis_index("wide"), NY)
    copies = [
        pltpu.make_async_copy(first, out1, sems.at[8]),
        pltpu.make_async_copy(second, out2, sems.at[9]),
    ]
    for copy in copies:
        copy.start()
    for steps in NEAR_STEPS:
        for dz, cols in zip(steps, columns_of(z, steps)):
            copies.append(
                pltpu.make_async_copy(acc.at[:, :, cols], out.at[:, :, cols], sems.at[dz])
            )
            copies[-1].start()
    for steps in REST_STEPS:
        columns = columns_of(z, steps)
        for plane in range(2):
            update(acc, stage, lhs, gathered, 1, steps, columns, 1 - core, (plane,))
            for dz, cols in zip(steps, columns):
                copies.append(
                    pltpu.make_async_copy(stage.at[plane, :, cols], out.at[plane, :, cols], sems.at[10 + 8 * plane + dz])
                )
                copies[-1].start(priority=plane)
    for copy in copies:
        copy.wait()


def body(inverse_first, inverse_second, coupling, head_rhs, panel_rows, trail_rhs):
    dma = pltpu.SemaphoreType.DMA
    held = pl.pallas_call(
        gather_kernel,
        out_shape=(
            pltpu.VMEM((2, 32, 64), F32),
            pltpu.VMEM((2, 32, 64), F32),
            pltpu.VMEM((2, 512, 1024), F32),
            pltpu.VMEM((2, 2, 512, 1024), BF16),
            pltpu.VMEM((2, 2, NZ, NY, NX, 32, 128), BF16),
        ),
        in_specs=[pl.BlockSpec(memory_space=pltpu.HBM)] * 6,
        out_specs=[pl.BlockSpec(memory_space=pltpu.VMEM)] * 5,
        scratch_shapes=[
            pltpu.VMEM((128, 512), F32),
            pltpu.VMEM((128, 512), F32),
            pltpu.VMEM((128, 512), F32),
            pltpu.VMEM((64, 1024), F32),
            pltpu.VMEM((512, 2048), BF16),
            pltpu.VMEM((8, 8, 512), F32),
            pltpu.VMEM((8, 8, 512), F32),
            pltpu.VMEM((8, 8, 512), F32),
            pltpu.VMEM((2, 128, 512), BF16),
            dma((6,)),
            dma((4,)),
            dma((2, 3)),
            dma((2, 14)),
        ],
        compiler_params=pltpu.CompilerParams(
            collective_id=0, has_side_effects=True, vmem_limit_bytes=24 << 20
        ),
        cost_estimate=pl.CostEstimate(flops=2 << 30, bytes_accessed=8 << 20, transcendentals=0),
    )(
        *(
            pltpu.with_memory_space_constraint(operand, pltpu.HBM)
            for operand in (
                inverse_first.reshape(128, 512),
                inverse_second.reshape(128, 512),
                jnp.transpose(coupling, (0, 2, 1)).reshape(128, 512),
                jnp.transpose(head_rhs, (0, 2, 1)).reshape(64, 1024),
                panel_rows,
                trail_rhs,
            )
        )
    )
    first, second, updated = pl.pallas_call(
        write_kernel,
        out_shape=(
            jax.ShapeDtypeStruct((2, 32, 64), F32),
            jax.ShapeDtypeStruct((2, 32, 64), F32),
            jax.ShapeDtypeStruct((2, 512, 1024), F32),
        ),
        in_specs=[pl.BlockSpec(memory_space=pltpu.VMEM)] * 5,
        out_specs=[pl.BlockSpec(memory_space=pltpu.HBM)] * 3,
        scratch_shapes=[pltpu.VMEM((2, 512, 1024), F32), dma((26,))],
        compiler_params=pltpu.CompilerParams(vmem_limit_bytes=16 << 20),
        cost_estimate=pl.CostEstimate(flops=2 << 30, bytes_accessed=4 << 20, transcendentals=0),
    )(*(pltpu.with_memory_space_constraint(value, pltpu.VMEM) for value in held))
    return jnp.transpose(first, (0, 2, 1)), jnp.transpose(second, (0, 2, 1)), updated


def solution(mesh):
    return jax.shard_map(
        body,
        mesh=mesh,
        in_specs=(
            P(None, "rows", None),
            P(None, "rows", None),
            P(None, None, "rows"),
            P(None, None, "wide"),
            P(("rows", "wide"), None),
            P(None, ("rows", "wide"), None),
        ),
        out_specs=(
            P(None, "rows", "wide"),
            P(None, "rows", "wide"),
            P(None, ("rows", "wide"), None),
        ),
        check_vma=False,
    )
```

```python
import functools

import jax
import jax.numpy as jnp
from jax import lax
from jax.experimental import pallas as pl
from jax.experimental.pallas import tpu as pltpu
from jax.sharding import PartitionSpec as P

MESH = pl.DeviceIdType.MESH
F32 = jnp.float32
BF16 = jnp.bfloat16
NX, NY, NZ = 4, 4, 8
NEAR = ((2, 2), (2, 1))
RELAY = (0,)
PLANE = sorted(
    ((i, j) for i in range(NX) for j in range(NY) if i or j),
    key=lambda p: -(min(p[0], NX - p[0]) + min(p[1], NY - p[1])),
)
SENT_FIRST, SENT, SENT_ON = range(3)
OVER_PLANE, ALONG_Z, SLABS, NEAR_ON, SLABS_ON, FAR, FAR_ON = 0, 1, 1, 4, 5, 6, 10
NT = (((1,), (1,)), ((), ()))
NN = (((1,), (0,)), ((), ()))


def split(value):
    high = value.astype(BF16)
    return high, (value - high.astype(F32)).astype(BF16)


def dot3(left, right, dims):
    (left_high, left_low), (right_high, right_low) = left, right
    dot = functools.partial(lax.dot_general, dimension_numbers=dims, preferred_element_type=F32)
    return dot(left_high, right_high) + (dot(left_low, right_high) + dot(left_high, right_low))


def swap(value):
    return pltpu.roll(value, 64, 1)


def first_lanes(shape):
    return lax.broadcasted_iota(jnp.int32, shape, 1) < 64


def solve(rhs, inverse):
    both = dot3(split(rhs), inverse, NT)
    top, low = both[:32], swap(both[32:])
    return jnp.where(first_lanes(top.shape), top - low, top + low)


class Net:
    def __init__(self, gathered, sems):
        self.g, self.sems = gathered, sems
        self.rows, self.wide = lax.axis_index("rows"), lax.axis_index("wide")
        self.x, self.core = lax.div(self.rows, 2), lax.rem(self.rows, 2)
        self.z, self.y = lax.div(self.wide, NY), lax.rem(self.wide, NY)

    def on_rows(self, j):
        return lax.rem(self.rows + j, 2 * NX), self.wide

    def on_plane(self, i, j):
        x, y = lax.rem(self.x + i, NX), lax.rem(self.y + j, NY)
        return 2 * x + self.core, self.z * NY + y

    def on_z(self, j):
        return self.rows, lax.rem(self.z + j, NZ) * NY + self.y

    def sibling(self):
        return self.rows + 1 - 2 * self.core, self.wide

    def copy(self, src, dst, half, sent, landed, to):
        send, recv = self.sems
        return pltpu.make_async_remote_copy(
            src_ref=src,
            dst_ref=dst,
            send_sem=send.at[half, sent],
            recv_sem=recv.at[half, landed],
            device_id=to,
            device_id_type=MESH,
        )

    def block(self, half, dz, i=0, j=0, core=None):
        x, y = lax.rem(self.x + (NX - i), NX), lax.rem(self.y + (NY - j), NY)
        return self.g.at[half, self.core if core is None else core, dz, y, x]

    def slab(self, half, dz):
        return self.g.at[half, self.core, dz]

    def far(self, half, near):
        return self.block(half, pl.ds(near + 1, NZ - 1 - 2 * near))

    def along_z(self, half, j):
        src, dst = self.block(half, 0), self.block(half, NZ - j)
        return self.copy(src, dst, half, SENT, ALONG_Z, self.on_z(j))

    def over_plane(self, half, i, j):
        ref = self.block(half, 0)
        return self.copy(ref, ref, half, SENT_FIRST, OVER_PLANE, self.on_plane(i, j))

    def slabs_along_z(self, half, step):
        for j in (step, NZ - step):
            src, dst = self.slab(half, 0), self.slab(half, NZ - j)
            yield self.copy(src, dst, half, SENT, SLABS + step, self.on_z(j))

    def far_over(self, half, near, i, j):
        ref = self.far(half, near)
        return self.copy(ref, ref, half, SENT, FAR + i, self.on_plane(i, j))

    def hand_on(self, half, ref, landed):
        self.copy(ref, ref, half, SENT_ON, landed, self.sibling()).start()

    def wait(self, half, blocks, sent=None, landed=None):
        z, y, x = blocks
        ref = self.g.at[half, self.core, pl.ds(0, z), pl.ds(0, y), pl.ds(0, x)]
        copy = self.copy(ref, ref, half, sent or 0, landed or 0, self.sibling())
        if landed is None:
            copy.wait_send()
        else:
            copy.wait_recv()


    def open(self, half, near):
        for j in far_steps(near):
            self.along_z(half, j).start()
        for i, j in PLANE:
            self.over_plane(half, i, j).start()

    def spread_plane(self, half, near):
        self.wait(half, (5, 3, 1), landed=OVER_PLANE)
        for step in range(1, (1 if half in RELAY else near) + 1):
            for copy in self.slabs_along_z(half, step):
                copy.start()
        self.hand_on(half, self.slab(half, 0), NEAR_ON)

    def relay(self, half, near):
        self.wait(half, (2, NY, NX), landed=SLABS + 1)
        for dz, way in ((NZ - 1, 1), (1, NZ - 1)):
            src, dst = self.slab(half, dz), self.slab(half, 2 * dz % NZ)
            self.copy(src, dst, half, SENT, SLABS + 2, self.on_z(way)).start()
        for dz in (1, NZ - 1):
            self.hand_on(half, self.slab(half, dz), NEAR_ON)

    def spread_z(self, half, near):
        self.wait(half, (NZ - 1 - 2 * near, 1, 1), landed=ALONG_Z)
        for i, j in [(2, 2), (1, 2), (3, 2), (0, 2), (2, 1), (1, 1), (3, 1), (0, 1), (2, 3), (1, 3), (3, 3), (0, 3), (2, 0), (1, 0), (3, 0)]:
            self.far_over(half, near, i, j).start()

    def take_slab(self, half, near, step):
        if step <= near:
            self.wait(half, (2, NY, NX), landed=SLABS + step)
            for dz in (step, NZ - step):
                self.hand_on(half, self.slab(half, dz), NEAR_ON if step == 1 else SLABS_ON)

    def take_slabs(self, half, near):
        for step in range(2 if half in RELAY else 1, near + 1):
            self.wait(half, (2, NY, NX), landed=SLABS + step)
            for dz in (step, NZ - step):
                self.hand_on(half, self.slab(half, dz), NEAR_ON if step == 1 else SLABS_ON)

    def take_far(self, half, near, i):
        count = NZ - 1 - 2 * near
        self.wait(half, (count, NY - 1 if i == 0 else NY, 1), landed=FAR + i)
        ref = self.g.at[half, self.core, pl.ds(near + 1, count), :, lax.rem(self.x + (NX - i), NX)]
        self.hand_on(half, ref, FAR_ON + i)

    def finish_near(self, half):
        self.wait(half, (3, NY, NX), landed=NEAR_ON)

    def finish_slabs(self, half, near):
        if near > 1:
            self.wait(half, (2 * near - 2, NY, NX), landed=SLABS_ON)

    def finish_far(self, half, near, i):
        self.wait(half, (NZ - 1 - 2 * near, NY, 1), landed=FAR_ON + i)

    def leave(self, half):
        self.wait(half, (5, 3, 1), sent=SENT_FIRST)
        self.wait(half, (NZ - 1, NY, NX), sent=SENT)
        self.wait(half, (NZ, NY, NX), sent=SENT_ON)


def far_steps(near):
    return sorted(range(near + 1, NZ - near), key=lambda j: -min(j, NZ - j))


def update(acc, out, lhs, gathered, half, steps, columns, core=None, planes=(0, 1)):
    right = jnp.concatenate(
        [
            jnp.concatenate([gathered[half, c, dz, :, x].reshape(128, 128) for dz in steps], 0)
            for c in (range(2) if core is None else [core])
            for x in range(NX)
        ],
        1,
    )
    for plane in planes:
        if core is None:
            left = lhs[half, plane]
        else:
            left = lhs[half, plane, :, pl.ds(pl.multiple_of(128 * NX * core, 128 * NX), 128 * NX)]
        product = lax.dot_general(left, right, NT, preferred_element_type=F32)
        for at, cols in enumerate(columns):
            out[plane, :, cols] = acc[plane, :, cols] + product[:, 128 * at : 128 * (at + 1)]


def columns_of(z, steps):
    return [pl.ds(pl.multiple_of(128 * lax.rem(z + dz, NZ), 128), 128) for dz in steps]


NEAR_STEPS, REST_STEPS = ((0, 1), (7,)), ((2, 3), (4, 5), (6,))


def gather_kernel(
    inv1_hbm, inv2_hbm, coup_hbm, head_hbm, panel_hbm, trail_hbm,
    out1, out2, acc, lhs, gathered,
    inv1, inv2, coup, head, panel, parts, sums, whole, inv2_split,
    local, sum_sems, send_sems, recv_sems,
):
    loads = [
        pltpu.make_async_copy(src, dst, local.at[i])
        for i, (src, dst) in enumerate(
            [
                (head_hbm, head),
                (inv1_hbm, inv1),
                (coup_hbm, coup),
                (inv2_hbm, inv2),
                (panel_hbm, panel),
                (trail_hbm, acc),
            ]
        )
    ]
    for load in loads[:3]:
        load.start()

    net = Net(gathered, (send_sems, recv_sems))
    rows, x, core = net.rows, net.x, net.core

    def stage(step, half, *more, other=False):
        near = NEAR[half][::-1] if other else NEAR[half]
        if near[0] == near[1]:
            step(half, near[0], *more)
        else:
            for at in range(2):
                pl.when(core == at)(functools.partial(step, half, near[at], *more))

    barrier = pltpu.get_barrier_semaphore()
    peers = [net.on_z(j) for j in far_steps(0)]
    peers += [net.on_plane(i, j) for i, j in PLANE if j]
    peers += [net.on_rows(j) for j in range(1, 2 * NX)]
    for peer in peers:
        pl.semaphore_signal(barrier, inc=1, device_id=peer, device_id_type=MESH)

    loads[0].wait()
    loads[1].wait()
    for load in loads[3:]:
        load.start()
    solved = solve(head[:, :512], split(inv1[...]))
    gathered[0, core, 0, net.y, x] = solved.astype(BF16)
    first = first_lanes(solved.shape)
    turned = swap(solved)
    out1[0] = solved[:, :64]
    out1[1] = turned[:, :64]
    loads[2].wait()
    left = jnp.concatenate([jnp.where(first, solved, -solved), turned], 0)
    parts[...] = dot3(split(left), split(coup[...]), NN).reshape(parts.shape)

    pl.semaphore_wait(barrier, len(peers))

    def reduce_copy(j):
        to = net.on_rows(j)
        return pltpu.make_async_remote_copy(
            src_ref=parts.at[to[0]],
            dst_ref=sums.at[j],
            send_sem=sum_sems.at[0],
            recv_sem=sum_sems.at[1],
            device_id=to,
            device_id_type=MESH,
        )

    def share_copy(j):
        ref = whole.at[rows]
        return pltpu.make_async_remote_copy(
            src_ref=ref,
            dst_ref=ref,
            send_sem=sum_sems.at[2],
            recv_sem=sum_sems.at[3],
            device_id=net.on_rows(j),
            device_id_type=MESH,
        )

    def all_seven(ref, at):
        ref = ref.at[pl.ds(1, 2 * NX - 1)]
        return pltpu.make_async_remote_copy(
            src_ref=ref,
            dst_ref=ref,
            send_sem=sum_sems.at[at],
            recv_sem=sum_sems.at[at + 1],
            device_id=net.sibling(),
            device_id_type=MESH,
        )

    order = (4, 3, 5, 2, 6, 1, 7)
    for j in order:
        reduce_copy(j).start()
    stage(net.open, 0)

    loads[4].wait()
    loads[3].wait()
    inv2_split[0], inv2_split[1] = split(inv2[...])

    all_seven(sums, 0).wait_recv()
    total = parts[rows]
    for j in range(1, 2 * NX):
        total += sums[j]
    whole[rows] = head[pl.ds(pl.multiple_of(8 * rows, 8), 8), 512:] - total
    for j in order:
        share_copy(j).start()

    stage(net.spread_plane, 0)
    stage(net.spread_z, 0)
    for half in range(2):
        for at in range(NX):
            base = 512 * half + 128 * at
            real = panel[:, base : base + 128].astype(F32)
            imag = panel[:, 1024 + base : 1024 + base + 128].astype(F32)
            head_lanes = first_lanes(real.shape)
            real_turned, imag_turned = swap(real), swap(imag)
            for c in range(2):
                k = (NX * c + at) * 128
                if c == 0:
                    plane0 = jnp.where(head_lanes, -real, imag_turned)
                    plane1 = jnp.where(head_lanes, -imag, -real_turned)
                else:
                    plane0 = jnp.where(head_lanes, -real_turned, imag)
                    plane1 = jnp.where(head_lanes, -imag_turned, -real)
                lhs[half, 0, :, k : k + 128] = plane0.astype(BF16)
                lhs[half, 1, :, k : k + 128] = plane1.astype(BF16)

    all_seven(whole, 2).wait_recv()
    solved = solve(whole[...].reshape(64, 512), (inv2_split[0], inv2_split[1]))
    gathered[1, core, 0, net.y, x] = solved.astype(BF16)
    stage(net.open, 1)
    out2[0] = solved[:, :64]
    out2[1] = swap(solved)[:, :64]

    def product(half, steps, *one):
        update(acc, acc, lhs, gathered, half, steps, columns_of(net.z, steps), *one)

    stage(net.relay, 0)
    stage(net.spread_z, 1)
    stage(net.spread_plane, 1)
    stage(net.take_slabs, 0)
    stage(net.take_far, 0, 0)
    stage(net.take_far, 0, 1)
    stage(net.take_far, 0, 3)
    stage(net.take_far, 0, 2)
    net.finish_near(0)
    loads[5].wait()
    product(0, (0, 1))
    stage(net.finish_slabs, 0, other=True)
    stage(net.finish_far, 0, 0, other=True)
    stage(net.finish_far, 0, 1, other=True)
    stage(net.finish_far, 0, 3, other=True)
    stage(net.finish_far, 0, 2, other=True)
    product(0, (7, 2))
    product(0, (6, 3))
    product(0, (5, 4))
    stage(net.take_slab, 1, 1)
    stage(net.take_far, 1, 0)
    stage(net.take_far, 1, 1)
    stage(net.take_far, 1, 3)
    stage(net.take_slab, 1, 2)
    stage(net.take_far, 1, 2)
    net.finish_near(1)
    product(1, (0, 1))
    product(1, (7,))
    for steps in REST_STEPS:
        product(1, steps, core)
    stage(net.finish_slabs, 1, other=True)
    stage(net.finish_far, 1, 0, other=True)
    stage(net.finish_far, 1, 1, other=True)
    stage(net.finish_far, 1, 3, other=True)
    stage(net.finish_far, 1, 2, other=True)
    all_seven(parts, 0).wait_send()
    all_seven(whole, 2).wait_send()
    net.leave(0)
    net.leave(1)


def write_kernel(first, second, acc, lhs, gathered, out1, out2, out, stage, sems):
    core, z = lax.rem(lax.axis_index("rows"), 2), lax.div(lax.axis_index("wide"), NY)
    copies = [
        pltpu.make_async_copy(first, out1, sems.at[8]),
        pltpu.make_async_copy(second, out2, sems.at[9]),
    ]
    for copy in copies:
        copy.start()
    for steps in NEAR_STEPS:
        for dz, cols in zip(steps, columns_of(z, steps)):
            copies.append(
                pltpu.make_async_copy(acc.at[:, :, cols], out.at[:, :, cols], sems.at[dz])
            )
            copies[-1].start()
    for steps in REST_STEPS:
        columns = columns_of(z, steps)
        for plane in range(2):
            update(acc, stage, lhs, gathered, 1, steps, columns, 1 - core, (plane,))
            for dz, cols in zip(steps, columns):
                copies.append(
                    pltpu.make_async_copy(stage.at[plane, :, cols], out.at[plane, :, cols], sems.at[10 + 8 * plane + dz])
                )
                copies[-1].start(priority=plane)
    for copy in copies:
        copy.wait()


def body(inverse_first, inverse_second, coupling, head_rhs, panel_rows, trail_rhs):
    dma = pltpu.SemaphoreType.DMA
    held = pl.pallas_call(
        gather_kernel,
        out_shape=(
            pltpu.VMEM((2, 32, 64), F32),
            pltpu.VMEM((2, 32, 64), F32),
            pltpu.VMEM((2, 512, 1024), F32),
            pltpu.VMEM((2, 2, 512, 1024), BF16),
            pltpu.VMEM((2, 2, NZ, NY, NX, 32, 128), BF16),
        ),
        in_specs=[pl.BlockSpec(memory_space=pltpu.HBM)] * 6,
        out_specs=[pl.BlockSpec(memory_space=pltpu.VMEM)] * 5,
        scratch_shapes=[
            pltpu.VMEM((128, 512), F32),
            pltpu.VMEM((128, 512), F32),
            pltpu.VMEM((128, 512), F32),
            pltpu.VMEM((64, 1024), F32),
            pltpu.VMEM((512, 2048), BF16),
            pltpu.VMEM((8, 8, 512), F32),
            pltpu.VMEM((8, 8, 512), F32),
            pltpu.VMEM((8, 8, 512), F32),
            pltpu.VMEM((2, 128, 512), BF16),
            dma((6,)),
            dma((4,)),
            dma((2, 3)),
            dma((2, 14)),
        ],
        compiler_params=pltpu.CompilerParams(
            collective_id=0, has_side_effects=True, vmem_limit_bytes=24 << 20
        ),
        cost_estimate=pl.CostEstimate(flops=2 << 30, bytes_accessed=8 << 20, transcendentals=0),
    )(
        *(
            pltpu.with_memory_space_constraint(operand, pltpu.HBM)
            for operand in (
                inverse_first.reshape(128, 512),
                inverse_second.reshape(128, 512),
                jnp.transpose(coupling, (0, 2, 1)).reshape(128, 512),
                jnp.transpose(head_rhs, (0, 2, 1)).reshape(64, 1024),
                panel_rows,
                trail_rhs,
            )
        )
    )
    first, second, updated = pl.pallas_call(
        write_kernel,
        out_shape=(
            jax.ShapeDtypeStruct((2, 32, 64), F32),
            jax.ShapeDtypeStruct((2, 32, 64), F32),
            jax.ShapeDtypeStruct((2, 512, 1024), F32),
        ),
        in_specs=[pl.BlockSpec(memory_space=pltpu.VMEM)] * 5,
        out_specs=[pl.BlockSpec(memory_space=pltpu.HBM)] * 3,
        scratch_shapes=[pltpu.VMEM((2, 512, 1024), F32), dma((26,))],
        compiler_params=pltpu.CompilerParams(vmem_limit_bytes=16 << 20),
        cost_estimate=pl.CostEstimate(flops=2 << 30, bytes_accessed=4 << 20, transcendentals=0),
    )(*(pltpu.with_memory_space_constraint(value, pltpu.VMEM) for value in held))
    return jnp.transpose(first, (0, 2, 1)), jnp.transpose(second, (0, 2, 1)), updated


def solution(mesh):
    return jax.shard_map(
        body,
        mesh=mesh,
        in_specs=(
            P(None, "rows", None),
            P(None, "rows", None),
            P(None, None, "rows"),
            P(None, None, "wide"),
            P(("rows", "wide"), None),
            P(None, ("rows", "wide"), None),
        ),
        out_specs=(
            P(None, "rows", "wide"),
            P(None, "rows", "wide"),
            P(None, ("rows", "wide"), None),
        ),
        check_vma=False,
    )
```
